32 devices in a mesh: group: 2 (over y), ctx: 16 (over z, x, core).
Axes of the slice: x: 2, y: 2, z: 4, core: 2. Of those that a mesh axis runs over, the one named last changes fastest.
Arguments:
- queries: bfloat16 [8192, 3072], P(('group', 'ctx')), parts along dimension 0, may hold values from -200 to 200
- key_matrix: bfloat16 [8192, 512], P(('group', 'ctx')), parts along dimension 0, may hold values from -4 to 4
- value_matrix: bfloat16 [8192, 512], P(('group', 'ctx')), parts along dimension 0, may hold values from -6 to 6
- tile_lists: int32 [64, 6], P(('group', 'ctx')), parts along dimension 0, may hold values from -1 to 31, as said below
- moe_tokens: bfloat16 [512, 3072], P(('group', 'ctx')), parts along dimension 0, may hold values from -6 to 6
- expert_ids: int32 [512, 2], P(('group', 'ctx')), parts along dimension 0, may hold values from 0 to 7, all different within a row; in each aligned block of 16 rows (0 to 15, 16 to 31, ...) at most 5 rows name the same one
- router_weight: bfloat16 [3072, 8], replicated, may hold values from -0.109375 to 0.109375
- gate_weight: bfloat16 [3072, 65536], P(None, 'ctx'), may hold values from -0.109375 to 0.109375
- up_weight: bfloat16 [3072, 65536], P(None, 'ctx'), may hold values from -0.109375 to 0.109375
- down_weight: bfloat16 [65536, 3072], P('ctx'), may hold values from -0.0625 to 0.0625
Outputs:
- attended: bfloat16 [8192, 3072], P(('group', 'ctx')), parts along dimension 0
- combined: bfloat16 [512, 3072], P(('group', 'ctx')), parts along dimension 0
The draws below stay inside these ranges and needn't reach their ends.
There are 2 independent parts, one for each index of `group`. The reference program is written for one: setup_inputs(seed, part) draws one part's arguments, and reference() takes and returns one part's arrays. A program takes and returns all parts, laid end to end along the dimension named above; an argument that names none is the same for every part. Nothing has to cross between parts.
Inputs may be any that keep to these rules, and one draw needn't show every extreme that they name: `tile_lists`: entry 0 of row b is b itself; the next entries are distinct key tiles before b whose positions lie on the same device as tile b or on one of the 4 devices before it; the rest of the row is -1. Some row lists 6 tiles. `expert_ids`: each token picks two different experts; among the 16 tokens of one device no expert is picked more than 5 times.
All inputs are finite; a program needn't handle non-finite values.
Results may differ from the reference program's by a relative error of at most 0.0049.
Values may be sent and summed in bfloat16 or wider, within the bound.
No kernel may reach another device: no remote copies, remote signals or barrier semaphores. Data moves between devices by JAX's collectives and lax.ppermute only.
A program may use at most 192 MiB of HBM per device.

```python
import math
import jax
import jax.numpy as jnp
import numpy as np
from jax import lax

TILE_POSITIONS = 128
HEAD_SIZE = 128
KEY_VALUE_HEADS = 4
QUERY_HEADS = 24
QUERY_PER_GROUP = 6
PRIOR_DEVICES = 4
MOST_LISTED = 6
S_DEV = 256
PROMPT_LENGTH = 4096
QUERY_TILE_COUNT = 32
D = 3072
FF = 8192
EXPERTS = 8
TOP = 2
TB = 16
CAP = 5
TOKENS_B = 256
N_CTX = 16


def shared_keys(key):
    base_offset = jax.random.normal(jax.random.fold_in(key, 101), (PROMPT_LENGTH, KEY_VALUE_HEADS * HEAD_SIZE), jnp.float32)
    return jnp.clip(base_offset, -4.0, 4.0)


def draw_key_matrix(key, part):
    base_offset = shared_keys(key)
    return base_offset.astype(jnp.bfloat16)


def draw_queries(key, part):
    key = jax.random.fold_in(key, 9)
    values = jnp.clip(jax.random.normal(key, (PROMPT_LENGTH, QUERY_HEADS * HEAD_SIZE), jnp.float32), -4.0, 4.0)
    return values.astype(jnp.bfloat16)


def draw_tile_lists(key, part):
    key = jax.random.fold_in(key, 5)
    tiles_per_device = S_DEV // TILE_POSITIONS
    span = (PRIOR_DEVICES + 1) * tiles_per_device
    devices_all = QUERY_TILE_COUNT // tiles_per_device
    block_ids = jnp.arange(QUERY_TILE_COUNT, dtype=jnp.int32)
    device_ids = block_ids // tiles_per_device
    offsets = jnp.arange(span, dtype=jnp.int32)
    candidate = (device_ids[:, None] - PRIOR_DEVICES) * tiles_per_device + offsets[None, :]
    usable = (candidate >= 0) & (candidate < block_ids[:, None])
    first_key, second_key, third_key = jax.random.split(key, 3)
    noise = jax.random.randint(first_key, (QUERY_TILE_COUNT, span), 0, 1 << 20)
    score = jnp.where(usable, noise * span + offsets[None, :], (1 << 20) * span + offsets[None, :])
    order = jnp.argsort(score, axis=1, stable=True)
    sorted_tiles = jnp.take_along_axis(candidate, order, axis=1)[:, :MOST_LISTED - 1]
    available = jnp.sum(usable.astype(jnp.int32), axis=1)
    device_level = jax.random.randint(second_key, (devices_all,), 0, MOST_LISTED)
    jitter = jax.random.randint(third_key, (QUERY_TILE_COUNT,), 0, 2)
    wanted = jnp.minimum(device_level[device_ids] + jitter, MOST_LISTED - 1)
    wanted = wanted.at[QUERY_TILE_COUNT - 1].set(MOST_LISTED - 1)
    extra = jnp.minimum(wanted, available)
    columns = jnp.arange(MOST_LISTED - 1, dtype=jnp.int32)
    rest = jnp.where(columns[None, :] < extra[:, None], sorted_tiles, -1)
    return jnp.concatenate([block_ids[:, None], rest], axis=1).astype(jnp.int32)


def levels(rng, dims, cuts, least, largest):
    def one(position, shards_of):
        draws = jax.random.uniform(jax.random.fold_in(jax.random.fold_in(rng, 6), position), (shards_of,), jnp.float32, least / len(cuts), largest / len(cuts))
        return jnp.repeat(jnp.exp(draws), dims[position] // shards_of).reshape((-1,) + (1,) * (len(dims) - position - 1))

    gain = one(*cuts[0])
    for cut in cuts[1:]:
        gain = gain * one(*cut)
    return gain


def routed_block(key, own, number, rows, count, top, bound, slope):
    order = jax.random.permutation(key, count)
    heavy_load, ordinary = load_shares(count, rows * top, bound, slope, True), load_shares(count, rows * top, bound, slope, False)
    places = jnp.arange(count)

    def named(lengths, rotation):
        used = int((lengths > 0).sum())
        fixed = max(1, used // 4)
        passed = fixed + (places - fixed + rotation * (used - fixed)) % max(1, count - fixed)
        return jnp.zeros((count,), jnp.int32).at[order[jnp.where(places < fixed, places, passed)]].set(jnp.asarray(lengths, jnp.int32))

    lengths = jnp.where(number % 4 == 0, named(heavy_load, number // 4), named(ordinary, number - number // 4 - 1))
    mixed = jax.random.permutation(jax.random.fold_in(own, 3), count)
    donor, receiver = mixed[0:count // 2 * 2:2], mixed[1:count // 2 * 2:2]
    room = jnp.minimum(lengths[donor] - 1, bound - lengths[receiver]) // 2
    room = jnp.where((donor == order[0]) | (receiver == order[0]) | (lengths[receiver] == 0), 0, jnp.maximum(room, 0))
    passed = jax.random.randint(jax.random.fold_in(own, 4), (count // 2,), 0, 1 << 20) % (room + 1)
    lengths = lengths.at[donor].add(-passed).at[receiver].add(passed)
    members = jnp.searchsorted(jnp.cumsum(lengths), jnp.arange(rows * top), side="right").astype(jnp.int32)
    table = members.reshape(top, rows).T
    table = table[jax.random.permutation(jax.random.fold_in(own, 1), rows)]
    rotation = jax.random.randint(jax.random.fold_in(own, 2), (rows, 1), 0, top)
    return jnp.take_along_axis(table, (jnp.arange(top)[None, :] + rotation) % top, axis=1)


def load_shares(number_of, total, limit, skew, full):
    weights = [(1 << 20) // math.isqrt(grade ** skew) + 1 for grade in range(1, number_of + 1)]
    largest = limit if full else min(limit, max(-(-total // number_of), total * weights[0] // sum(weights)))
    least = 1 if total - largest >= number_of - 1 else 0
    counts, spare = [largest] + [least] * (number_of - 1), total - largest - least * (number_of - 1)
    while spare > 0:
        free = [i for i in range(1, number_of) if counts[i] < largest] or [i for i in range(1, number_of) if counts[i] < limit]
        mass, left = sum([weights[i] for i in free]), spare
        for i in free:
            more = min(limit - counts[i], max(1, left * weights[i] // mass), spare)
            counts[i] = counts[i] + more
            spare = spare - more
    return np.array(counts)


def bell_draw(own_key, dims, width, limit, pieces=(), kind=jnp.bfloat16):
    values = jax.random.normal(own_key, dims, jnp.float32) * width
    if len(pieces) > 0:
        values = levels(own_key, dims, pieces, -0.22, 0.18) * values
    return jnp.clip(values, min=-limit, max=limit).astype(kind)


def setup_inputs(seed: int = 0, part: int = 0) -> dict:
    splits = jax.random.split(jax.random.key(seed), 11)
    part_keys = jax.random.split(jax.random.fold_in(splits[10], part), 11)
    queries = draw_queries(jax.random.fold_in(jax.random.fold_in(splits[10], part), 71), part)
    key_matrix = draw_key_matrix(jax.random.fold_in(jax.random.fold_in(splits[10], part), 71), part)
    value_matrix = bell_draw(part_keys[2], (PROMPT_LENGTH, KEY_VALUE_HEADS * HEAD_SIZE), 1.0, 6.0, ((0, 16),))
    tile_lists = draw_tile_lists(jax.random.fold_in(jax.random.fold_in(splits[10], part), 71), part)
    moe_tokens = bell_draw(part_keys[4], (TOKENS_B, D), 1.0, 6.0, ((0, 16),))
    expert_ids_keys = jax.random.split(jax.random.fold_in(part_keys[5], 1), TOKENS_B // TB)
    expert_ids_turns = jax.random.permutation(jax.random.fold_in(part_keys[5], 3), TOKENS_B // TB)
    expert_ids = jax.vmap(lambda own, number: routed_block(jax.random.fold_in(part_keys[5], 2), own, number, TB, EXPERTS, TOP, CAP, 2))(expert_ids_keys, expert_ids_turns).reshape((TOKENS_B, TOP))
    router_weight = bell_draw(splits[6], (D, EXPERTS), D ** -0.5, 0.109375)
    gate_weight = bell_draw(splits[7], (D, EXPERTS * FF), D ** -0.5, 0.109375, ((1, 16),))
    up_weight = bell_draw(splits[8], (D, EXPERTS * FF), D ** -0.5, 0.109375, ((1, 16),))
    down_weight = bell_draw(splits[9], (EXPERTS * FF, D), FF ** -0.5, 0.0625, ((0, 16),))
    return {"queries": queries, "key_matrix": key_matrix, "value_matrix": value_matrix, "tile_lists": tile_lists, "moe_tokens": moe_tokens, "expert_ids": expert_ids, "router_weight": router_weight, "gate_weight": gate_weight, "up_weight": up_weight, "down_weight": down_weight}


masked_value = -1e30


def attention(queries, key_matrix, value_matrix, tile_lists):
    query_tile_rows = queries.reshape(QUERY_TILE_COUNT, TILE_POSITIONS, KEY_VALUE_HEADS, QUERY_PER_GROUP, HEAD_SIZE)
    key_tile_rows = key_matrix.reshape(QUERY_TILE_COUNT, TILE_POSITIONS, KEY_VALUE_HEADS, HEAD_SIZE)
    value_tile_rows = value_matrix.reshape(QUERY_TILE_COUNT, TILE_POSITIONS, KEY_VALUE_HEADS, HEAD_SIZE)
    offsets = jnp.arange(TILE_POSITIONS, dtype=jnp.int32)

    def attend_block(inputs):
        block_index, query_tile, listed = inputs
        usable = listed >= 0
        clamped_list = jnp.where(usable, listed, 0).astype(jnp.int32)
        key_portion = jnp.take(key_tile_rows, clamped_list, axis=0).reshape(MOST_LISTED * TILE_POSITIONS, KEY_VALUE_HEADS, HEAD_SIZE)
        value_portion = jnp.take(value_tile_rows, clamped_list, axis=0).reshape(MOST_LISTED * TILE_POSITIONS, KEY_VALUE_HEADS, HEAD_SIZE)
        key_pos = (clamped_list[:, None] * TILE_POSITIONS + offsets[None, :]).reshape(MOST_LISTED * TILE_POSITIONS)
        key_usable = jnp.repeat(usable, TILE_POSITIONS)
        query_pos = block_index * TILE_POSITIONS + offsets
        allowed = key_usable[None, :] & (key_pos[None, :] <= query_pos[:, None])
        scores = jnp.einsum('qhgd,khd->hgqk', query_tile.astype(jnp.float32), key_portion.astype(jnp.float32)) * (HEAD_SIZE ** -0.5)
        scores = jnp.where(allowed[None, None], scores, masked_value)
        highest = jnp.max(scores, axis=-1, keepdims=True)
        weights = jnp.exp(scores - highest)
        total = jnp.sum(weights, axis=-1, keepdims=True)
        rounded = weights.astype(jnp.bfloat16)
        summed = jnp.einsum('hgqk,khd->qhgd', rounded.astype(jnp.float32), value_portion.astype(jnp.float32))
        result = summed / jnp.transpose(total, (2, 0, 1, 3))
        return result.reshape(TILE_POSITIONS, QUERY_HEADS * HEAD_SIZE).astype(jnp.bfloat16)

    block_ids = jnp.arange(QUERY_TILE_COUNT, dtype=jnp.int32)
    outputs = lax.map(attend_block, (block_ids, query_tile_rows, tile_lists))
    return outputs.reshape(PROMPT_LENGTH, QUERY_HEADS * HEAD_SIZE)


def mixture(moe_tokens, expert_ids, router_weight, gate_weight, up_weight, down_weight):
    logits = jnp.dot(moe_tokens, router_weight, preferred_element_type=jnp.float32)
    picked = jnp.take_along_axis(logits, expert_ids, axis=1)
    gate_shares = jax.nn.softmax(picked, axis=1)
    flat_ids = expert_ids.reshape(-1).astype(jnp.int32)
    picks_total = flat_ids.shape[0]
    onehot = (flat_ids[:, None] == jnp.arange(EXPERTS, dtype=jnp.int32)[None, :]).astype(jnp.int32)
    before = jnp.cumsum(onehot, axis=0) - onehot
    slot_index = jnp.take_along_axis(before, flat_ids[:, None], axis=1)[:, 0].astype(jnp.int32)
    owners = (jnp.arange(picks_total, dtype=jnp.int32) // TOP).astype(jnp.int32)
    table = jnp.zeros((EXPERTS, N_CTX * CAP), jnp.int32).at[flat_ids, slot_index].set(owners)
    gate_stack = jnp.transpose(gate_weight.reshape(D, EXPERTS, FF), (1, 0, 2))
    up_stack = jnp.transpose(up_weight.reshape(D, EXPERTS, FF), (1, 0, 2))
    down_stack = down_weight.reshape(EXPERTS, FF, D)

    def run_expert(inputs):
        table_row, gate_part, up_part, down_part = inputs
        rows = jnp.take(moe_tokens, table_row, axis=0)
        gate_value = jnp.dot(rows, gate_part, preferred_element_type=jnp.float32)
        up_value = jnp.dot(rows, up_part, preferred_element_type=jnp.float32)
        hidden = (jax.nn.silu(gate_value) * up_value).astype(jnp.bfloat16)
        return jnp.dot(hidden, down_part, preferred_element_type=jnp.float32)

    outputs = lax.map(run_expert, (table, gate_stack, up_stack, down_stack))
    chosen = outputs[flat_ids, slot_index].reshape(TOKENS_B, TOP, D)
    return jnp.sum(gate_shares[:, :, None] * chosen, axis=1).astype(jnp.bfloat16)


def reference(queries, key_matrix, value_matrix, tile_lists, moe_tokens, expert_ids, router_weight, gate_weight, up_weight, down_weight):
    attended = attention(queries, key_matrix, value_matrix, tile_lists)
    combined = mixture(moe_tokens, expert_ids, router_weight, gate_weight, up_weight, down_weight)
    return (attended, combined)
```

```python
import functools

import jax
import jax.numpy as jnp
from jax import lax
from jax.experimental import pallas as pl
from jax.experimental.pallas import tpu as pltpu
from jax.sharding import PartitionSpec as P

TILE_POSITIONS = 128
HEAD_SIZE = 128
KEY_VALUE_HEADS = 4
QUERY_HEADS = 24
QUERY_PER_GROUP = 6
PRIOR_DEVICES = 4
MOST_LISTED = 6
D = 3072
EXPERTS = 8
TOP = 2
CAP = 5

PARTS = 24
PART_WIDTH = D // PARTS
HIDDEN_CHUNK = 512
LOG2_E = 1.4426950408889634
MIB = 2**20

WINDOW_SOURCES = ((1, 4, 2, 5, 0), (1, 5, 2, 3, 0), (1, 4, 2, 5, 0), (1, 5, 2, 3, 0))


def exchanged(x, by):
    devices = lax.axis_size("ctx")
    return lax.ppermute(x, "ctx", [(i, i ^ by) for i in range(devices)])


def same_core_exchange(x):
    devices = lax.axis_size("ctx")
    groups = [[core + 2 * i for i in range(devices // 2)] for core in range(2)]
    return lax.all_to_all(x, "ctx", split_axis=0, concat_axis=0, tiled=True, axis_index_groups=groups)


def pack_kernel(ids_ref, tokens_ref, out_ref, rows_ref, count_ref):
    tokens = tokens_ref.shape[0]
    for part in range(PARTS):
        columns = slice(part * PART_WIDTH, (part + 1) * PART_WIDTH)
        rows_ref[pl.ds(part, tokens, stride=PARTS), :] = tokens_ref[:, columns].astype(jnp.float32)
    out_ref[...] = jnp.zeros_like(out_ref)
    for expert in range(EXPERTS):
        count_ref[expert] = 0
    for token in range(tokens):
        row = rows_ref[token * PARTS : (token + 1) * PARTS, :].astype(jnp.bfloat16)
        for pick in range(TOP):
            expert = ids_ref[token, pick]
            slot = count_ref[expert]
            count_ref[expert] = slot + 1
            out_ref[expert, slot] = row


def pack(moe_tokens, expert_ids):
    tokens = moe_tokens.shape[0]
    return pl.pallas_call(
        pack_kernel,
        out_shape=jax.ShapeDtypeStruct((EXPERTS, CAP, PARTS, PART_WIDTH), jnp.bfloat16),
        in_specs=[pl.BlockSpec(memory_space=pltpu.SMEM), pl.BlockSpec(memory_space=pltpu.VMEM)],
        out_specs=pl.BlockSpec(memory_space=pltpu.VMEM),
        scratch_shapes=[
            pltpu.VMEM((tokens * PARTS, PART_WIDTH), jnp.float32),
            pltpu.SMEM((EXPERTS,), jnp.int32),
        ],
        name="pack",
    )(expert_ids, moe_tokens)


def shares_kernel(ids_ref, tokens_ref, router_ref, out_ref):
    logits = lax.dot_general(
        tokens_ref[...], router_ref[...], (((1,), (1,)), ((), ())), preferred_element_type=jnp.float32
    )
    places = lax.broadcasted_iota(jnp.int32, logits.shape, 1)
    ids = ids_ref[...]
    picked = [
        jnp.sum(jnp.where(places == ids[:, pick : pick + 1], logits, 0.0), axis=1, keepdims=True)
        for pick in range(TOP)
    ]
    top = jnp.maximum(picked[0], picked[1])
    weights = [jnp.exp(value - top) for value in picked]
    total = weights[0] + weights[1]
    out_ref[...] = jnp.concatenate([weights[0] / total, weights[1] / total], axis=1)


def shares(moe_tokens, expert_ids, router_weight):
    return pl.pallas_call(
        shares_kernel,
        out_shape=jax.ShapeDtypeStruct(expert_ids.shape, jnp.float32),
        in_specs=[pl.BlockSpec(memory_space=pltpu.VMEM)] * 3,
        out_specs=pl.BlockSpec(memory_space=pltpu.VMEM),
        name="shares",
    )(expert_ids, moe_tokens, router_weight.T)


def experts_kernel(near_ref, far_ref, gate_ref, up_ref, down_ref, mine_ref, other_ref, parts_ref, rows_ref, sums_ref, down_vmem, sems):
    senders = near_ref.shape[0]
    slots = senders * CAP
    count = 2 * slots
    hidden_units = gate_ref.shape[1]
    chunks = hidden_units // HIDDEN_CHUNK
    depth = down_vmem.shape[0]

    def down_copy(chunk, slot):
        return pltpu.make_async_copy(
            down_ref.at[pl.ds(chunk * HIDDEN_CHUNK, HIDDEN_CHUNK)], down_vmem.at[slot], sems.at[slot]
        )

    for chunk in range(min(depth, chunks)):
        down_copy(chunk, chunk).start()
    for place, ref in enumerate((near_ref, far_ref)):

        def unpack(i, carry, place=place, ref=ref):
            first = pl.multiple_of((place * senders + i) * CAP * PARTS, 8)
            parts_ref[pl.ds(first, CAP * PARTS), :] = (
                ref[i].astype(jnp.float32).reshape(CAP * PARTS, PART_WIDTH)
            )
            return carry

        lax.fori_loop(0, senders, unpack, 0)
    for part in range(PARTS):
        columns = slice(part * PART_WIDTH, (part + 1) * PART_WIDTH)
        rows_ref[:, columns] = parts_ref[pl.ds(part, count, stride=PARTS), :].astype(jnp.bfloat16)

    def work(chunk, first):
        columns = pl.ds(pl.multiple_of(chunk * HIDDEN_CHUNK, HIDDEN_CHUNK), HIDDEN_CHUNK)
        gate_value = jnp.dot(rows_ref[...], gate_ref[:, columns], preferred_element_type=jnp.float32)
        up_value = jnp.dot(rows_ref[...], up_ref[:, columns], preferred_element_type=jnp.float32)
        hidden = (gate_value / (1.0 + jnp.exp(-gate_value)) * up_value).astype(jnp.bfloat16)
        slot = lax.rem(chunk, depth)
        down_copy(chunk, slot).wait()
        product = jnp.dot(hidden, down_vmem[slot], preferred_element_type=jnp.float32)
        if first:
            sums_ref[...] = product
        else:
            sums_ref[...] += product

        @pl.when(chunk + depth < chunks)
        def _():
            down_copy(chunk + depth, slot).start()

    work(0, True)

    def step(chunk, carry):
        work(chunk, False)
        return carry

    lax.fori_loop(1, chunks, step, 0)
    for part in range(PARTS):
        columns = slice(part * PART_WIDTH, (part + 1) * PART_WIDTH)
        parts_ref[pl.ds(part, count, stride=PARTS), :] = sums_ref[:, columns]

    def give(i, carry):
        first = pl.multiple_of(i * CAP * PARTS, 8)
        mine_ref[i] = parts_ref[pl.ds(first, CAP * PARTS), :].reshape(CAP, PARTS, PART_WIDTH)
        second = pl.multiple_of((senders + i) * CAP * PARTS, 8)
        other_ref[i] = (
            parts_ref[pl.ds(second, CAP * PARTS), :].reshape(CAP, PARTS, PART_WIDTH).astype(jnp.bfloat16)
        )
        return carry

    lax.fori_loop(0, senders, give, 0)


def experts(near, far, gate_weight, up_weight, down_weight):
    senders = near.shape[0]
    count = 2 * senders * CAP
    vmem = pl.BlockSpec(memory_space=pltpu.VMEM)
    hidden_units = gate_weight.shape[1]
    depth = min(3, hidden_units // HIDDEN_CHUNK)
    return pl.pallas_call(
        experts_kernel,
        out_shape=(
            jax.ShapeDtypeStruct(near.shape, jnp.float32),
            jax.ShapeDtypeStruct(near.shape, jnp.bfloat16),
        ),
        in_specs=[vmem, vmem, vmem, vmem, pl.BlockSpec(memory_space=pl.ANY)],
        out_specs=(vmem, vmem),
        scratch_shapes=[
            pltpu.VMEM((count * PARTS, PART_WIDTH), jnp.float32),
            pltpu.VMEM((count, D), jnp.bfloat16),
            pltpu.VMEM((count, D), jnp.float32),
            pltpu.VMEM((depth, HIDDEN_CHUNK, D), jnp.bfloat16),
            pltpu.SemaphoreType.DMA((depth,)),
        ],
        compiler_params=pltpu.CompilerParams(vmem_limit_bytes=VMEM_EXPERTS),
        name="experts",
    )(near, far, gate_weight, up_weight, down_weight)


VMEM_EXPERTS = 62 * MIB


def combine_kernel(ids_ref, shares_ref, back_ref, out_ref, rows_ref, count_ref):
    tokens = out_ref.shape[0]
    holders = back_ref.shape[0] // EXPERTS
    for expert in range(EXPERTS):
        count_ref[expert] = 0
    for token in range(tokens):
        total = None
        for pick in range(TOP):
            expert = ids_ref[token, pick]
            slot = count_ref[expert]
            count_ref[expert] = slot + 1
            value = back_ref[expert * holders, slot].astype(jnp.float32)
            for holder in range(1, holders):
                value += back_ref[expert * holders + holder, slot].astype(jnp.float32)
            value = shares_ref[token, pick] * value
            total = value if total is None else total + value
        rows_ref[token * PARTS : (token + 1) * PARTS, :] = total
    for part in range(PARTS):
        columns = slice(part * PART_WIDTH, (part + 1) * PART_WIDTH)
        out_ref[:, columns] = rows_ref[pl.ds(part, tokens, stride=PARTS), :].astype(jnp.bfloat16)


def combine(expert_ids, gate_shares, back):
    tokens = expert_ids.shape[0]
    smem = pl.BlockSpec(memory_space=pltpu.SMEM)
    vmem = pl.BlockSpec(memory_space=pltpu.VMEM)
    return pl.pallas_call(
        combine_kernel,
        out_shape=jax.ShapeDtypeStruct((tokens, D), jnp.bfloat16),
        in_specs=[smem, smem, vmem],
        out_specs=vmem,
        scratch_shapes=[
            pltpu.VMEM((tokens * PARTS, PART_WIDTH), jnp.float32),
            pltpu.SMEM((EXPERTS,), jnp.int32),
        ],
        compiler_params=pltpu.CompilerParams(vmem_limit_bytes=16 * MIB),
        name="combine",
    )(expert_ids, gate_shares, back)


def attention_kernel(
    place_ref, lists_ref, query_ref, key_ref, value_ref, b1, b2, b3, b4, b5, out_ref, window, stacked, scores, weights, sems
):
    tile, head = pl.program_id(0), pl.program_id(1)
    copies = [
        pltpu.make_async_copy(key_ref, window.at[0, 0], sems.at[0]),
        pltpu.make_async_copy(value_ref, window.at[0, 1], sems.at[1]),
    ] + [pltpu.make_async_copy(ref, window.at[i + 1], sems.at[i + 2]) for i, ref in enumerate((b1, b2, b3, b4, b5))]

    @pl.when((tile == 0) & (head == 0))
    def _():
        for copy in copies:
            copy.start()
        for copy in copies:
            copy.wait()

    tiles_here = key_ref.shape[0] // TILE_POSITIONS
    first_tile = place_ref[0]
    for group in range(QUERY_PER_GROUP):
        stacked[group * TILE_POSITIONS : (group + 1) * TILE_POSITIONS, :] = query_ref[
            :, group * HEAD_SIZE : (group + 1) * HEAD_SIZE
        ]
    columns = pl.ds(pl.multiple_of(head * HEAD_SIZE, HEAD_SIZE), HEAD_SIZE)
    listed_count = jnp.int32(1)
    for entry in range(1, MOST_LISTED):
        listed_count += (lists_ref[tile, entry] >= 0).astype(jnp.int32)

    def fetch(which, entry):
        relative = jnp.clip(lists_ref[tile, entry] - first_tile, 0, (PRIOR_DEVICES + 1) * tiles_here - 1)
        source = place_ref[1 + lax.div(relative, tiles_here)]
        first = pl.multiple_of(lax.rem(relative, tiles_here) * TILE_POSITIONS, TILE_POSITIONS)
        return window[source, which, pl.ds(first, TILE_POSITIONS), columns]

    def attend(listed):
        keys = jnp.concatenate([fetch(0, entry) for entry in range(listed)], axis=0)
        width = listed * TILE_POSITIONS
        scores[:, :width] = lax.dot_general(
            stacked[...], keys, (((1,), (1,)), ((), ())), preferred_element_type=jnp.float32
        )
        totals = []
        for group in range(QUERY_PER_GROUP):
            rows = slice(group * TILE_POSITIONS, (group + 1) * TILE_POSITIONS)
            row_place = lax.broadcasted_iota(jnp.int32, (TILE_POSITIONS, TILE_POSITIONS), 0)
            column_place = lax.broadcasted_iota(jnp.int32, (TILE_POSITIONS, TILE_POSITIONS), 1)
            own = jnp.where(column_place <= row_place, scores[rows, :TILE_POSITIONS], -1e30)
            blocks = [own] + [
                scores[rows, entry * TILE_POSITIONS : (entry + 1) * TILE_POSITIONS] for entry in range(1, listed)
            ]
            top = blocks[0]
            for block in blocks[1:]:
                top = jnp.maximum(top, block)
            top = jnp.max(top, axis=1, keepdims=True)
            total = None
            for entry, block in enumerate(blocks):
                weight = jnp.exp2((block - top) * (HEAD_SIZE**-0.5 * LOG2_E))
                total = weight if total is None else total + weight
                weights[rows, entry * TILE_POSITIONS : (entry + 1) * TILE_POSITIONS] = weight.astype(jnp.bfloat16)
            totals.append(jnp.sum(total, axis=1, keepdims=True))
        values = jnp.concatenate([fetch(1, entry) for entry in range(listed)], axis=0)
        summed = jnp.dot(weights[:, :width], values, preferred_element_type=jnp.float32)
        for group in range(QUERY_PER_GROUP):
            rows = slice(group * TILE_POSITIONS, (group + 1) * TILE_POSITIONS)
            out_ref[:, group * HEAD_SIZE : (group + 1) * HEAD_SIZE] = (summed[rows] / totals[group]).astype(jnp.bfloat16)

    for listed in range(1, MOST_LISTED + 1):
        pl.when(listed_count == listed)(functools.partial(attend, listed))


def attention(place, tile_lists, queries, keys, values, blocks):
    rows_here = queries.shape[0]
    tiles_here = rows_here // TILE_POSITIONS
    group_width = QUERY_PER_GROUP * HEAD_SIZE
    anywhere = pl.BlockSpec(memory_space=pl.ANY)
    query_spec = pl.BlockSpec((TILE_POSITIONS, group_width), lambda tile, head, *_: (tile, head))
    stacked_rows = QUERY_PER_GROUP * TILE_POSITIONS
    most = MOST_LISTED * TILE_POSITIONS
    return pl.pallas_call(
        attention_kernel,
        out_shape=jax.ShapeDtypeStruct(queries.shape, jnp.bfloat16),
        grid_spec=pltpu.PrefetchScalarGridSpec(
            num_scalar_prefetch=2,
            grid=(tiles_here, KEY_VALUE_HEADS),
            in_specs=[query_spec] + [anywhere] * 7,
            out_specs=query_spec,
            scratch_shapes=[
                pltpu.VMEM((6, 2, rows_here, KEY_VALUE_HEADS * HEAD_SIZE), jnp.bfloat16),
                pltpu.VMEM((stacked_rows, HEAD_SIZE), jnp.bfloat16),
                pltpu.VMEM((stacked_rows, most), jnp.float32),
                pltpu.VMEM((stacked_rows, most), jnp.bfloat16),
                pltpu.SemaphoreType.DMA((7,)),
            ],
        ),
        compiler_params=pltpu.CompilerParams(vmem_limit_bytes=24 * MIB),
        name="attention",
    )(place, tile_lists, queries, keys, values, *blocks)


def shards(
    queries,
    key_matrix,
    value_matrix,
    tile_lists,
    moe_tokens,
    expert_ids,
    router_weight,
    gate_weight,
    up_weight,
    down_weight,
):
    devices = lax.axis_size("ctx")
    me = lax.axis_index("ctx")
    packed = pack(moe_tokens, expert_ids)
    pairs_per_expert = devices // (2 * EXPERTS)
    if pairs_per_expert > 1:
        packed = jnp.repeat(packed, pairs_per_expert, axis=0)
    near = same_core_exchange(packed)
    own = jnp.stack([key_matrix, value_matrix])
    before = lax.ppermute(own, "ctx", [(i, i + 4) for i in range(devices - 4)])
    far = exchanged(near, 1)
    across = exchanged(jnp.where(me % 4 < 2, own, before), 2)
    gate_shares = shares(moe_tokens, expert_ids, router_weight)
    mine, other = experts(near, far, gate_weight, up_weight, down_weight)
    summed = (mine + exchanged(other, 1).astype(jnp.float32)).astype(jnp.bfloat16)
    back = same_core_exchange(summed)
    blocks = [before, across] + [exchanged(x, 1) for x in (own, before, across)]
    tiles_here = queries.shape[0] // TILE_POSITIONS
    sources = jnp.take(jnp.array(WINDOW_SOURCES, jnp.int32), me % 4, axis=0)
    place = jnp.concatenate([((me - PRIOR_DEVICES) * tiles_here).astype(jnp.int32)[None], sources])
    attended = attention(place, tile_lists, queries, key_matrix, value_matrix, blocks)
    combined = combine(expert_ids, gate_shares, back)
    return (attended, combined)


def solution(mesh):
    split = P(("group", "ctx"), None)
    placed = (split, split, split, split, split, split, P(), P(None, "ctx"), P(None, "ctx"), P("ctx", None))
    return jax.shard_map(shards, mesh=mesh, in_specs=placed, out_specs=(split, split), check_vma=False)
```

```python
import functools

import jax
import jax.numpy as jnp
from jax import lax
from jax.experimental import pallas as pl
from jax.experimental.pallas import tpu as pltpu
from jax.sharding import PartitionSpec as P

TILE_POSITIONS = 128
HEAD_SIZE = 128
KEY_VALUE_HEADS = 4
QUERY_HEADS = 24
QUERY_PER_GROUP = 6
PRIOR_DEVICES = 4
MOST_LISTED = 6
D = 3072
EXPERTS = 8
TOP = 2
CAP = 5

PARTS = 24
PART_WIDTH = D // PARTS
PIECES = 4
FIRST_HELD = D // 4
HIDDEN_CHUNK = 512
HEADS_PER_STEP = 2
LOG2_E = 1.4426950408889634
MIB = 2**20

WINDOW_SOURCES = ((2, 5, 1, 4, 0), (2, 4, 1, 3, 0))


def in_vmem(x):
    return pltpu.with_memory_space_constraint(x, pltpu.VMEM)


def in_hbm(x):
    return pltpu.with_memory_space_constraint(x, pltpu.HBM)


def exchanged(x, by):
    devices = lax.axis_size("ctx")
    return lax.ppermute(x, "ctx", [(i, i ^ by) for i in range(devices)])


def passed_along(x, by):
    devices = lax.axis_size("ctx")
    return lax.ppermute(x, "ctx", [(i, (i + by) % devices) for i in range(devices)])


def same_core_exchange(x):
    devices = lax.axis_size("ctx")
    groups = [[core + 2 * i for i in range(devices // 2)] for core in range(2)]
    return lax.all_to_all(x, "ctx", split_axis=0, concat_axis=0, tiled=True, axis_index_groups=groups)


def pack_kernel(ids_ref, base_ref, tokens_ref, keep_ref, send_ref, rows_ref, slots_ref, count_ref):
    tokens = tokens_ref.shape[0]
    base = base_ref[0]
    for part in range(PARTS):
        columns = slice(part * PART_WIDTH, (part + 1) * PART_WIDTH)
        rows_ref[pl.ds(part, tokens, stride=PARTS), :] = tokens_ref[:, columns].astype(jnp.float32)
    slots_ref[...] = jnp.zeros_like(slots_ref)
    for expert in range(EXPERTS):
        count_ref[expert] = 0
    for token in range(tokens):
        row = rows_ref[token * PARTS : (token + 1) * PARTS, :].astype(jnp.bfloat16)
        for pick in range(TOP):
            expert = ids_ref[pick, token]
            slot = count_ref[expert]
            count_ref[expert] = slot + 1
            place = lax.bitwise_xor(expert, base)
            slots_ref[lax.bitwise_and(place, 1), lax.shift_right_logical(place, 1), slot] = row
    keep_ref[...] = slots_ref[0]
    send_ref[...] = slots_ref[1]


def pack(ids, base, moe_tokens):
    tokens = moe_tokens.shape[0]
    smem = pl.BlockSpec(memory_space=pltpu.SMEM)
    vmem = pl.BlockSpec(memory_space=pltpu.VMEM)
    half = (EXPERTS // 2, CAP, PARTS, PART_WIDTH)
    return pl.pallas_call(
        pack_kernel,
        out_shape=(jax.ShapeDtypeStruct(half, jnp.bfloat16),) * 2,
        in_specs=[smem, smem, vmem],
        out_specs=(vmem, vmem),
        scratch_shapes=[
            pltpu.VMEM((tokens * PARTS, PART_WIDTH), jnp.float32),
            pltpu.VMEM((2,) + half, jnp.bfloat16),
            pltpu.SMEM((EXPERTS,), jnp.int32),
        ],
        compiler_params=pltpu.CompilerParams(vmem_limit_bytes=4 * MIB),
        name="pack",
    )(in_hbm(ids), base, in_hbm(moe_tokens))


def join_kernel(keep_ref, came_ref, mark_ref, *out_refs):
    for place, ref in enumerate(out_refs[:-1]):
        ref[0] = keep_ref[place]
        ref[1] = came_ref[place]
    out_refs[-1][...] = mark_ref[...] + 1


def join(keep, came, mark):
    vmem = pl.BlockSpec(memory_space=pltpu.VMEM)
    shape = jax.ShapeDtypeStruct((2,) + keep.shape[1:], keep.dtype)
    count = keep.shape[0]
    return pl.pallas_call(
        join_kernel,
        out_shape=(shape,) * count + (jax.ShapeDtypeStruct(mark.shape, mark.dtype),),
        in_specs=[vmem] * 3,
        out_specs=(vmem,) * (count + 1),
        compiler_params=pltpu.CompilerParams(vmem_limit_bytes=4 * MIB),
        name="join",
    )(keep, came, mark)


def merge_kernel(mark_ref, *refs):
    for place, ref in enumerate(refs[:-1]):
        refs[-1][2 * place : 2 * place + 2] = ref[...]


def merge(mark, pieces):
    vmem = pl.BlockSpec(memory_space=pltpu.VMEM)
    return pl.pallas_call(
        merge_kernel,
        out_shape=jax.ShapeDtypeStruct((2 * len(pieces),) + pieces[0].shape[1:], pieces[0].dtype),
        in_specs=[vmem] * (1 + len(pieces)),
        out_specs=vmem,
        compiler_params=pltpu.CompilerParams(vmem_limit_bytes=4 * MIB),
        name="merge",
    )(mark, *pieces)


def hold_kernel(first, mark_ref, gate_ref, next_ref, held_ref, sems):
    rows = held_ref.shape[0] // PIECES
    copies = [
        pltpu.make_async_copy(
            gate_ref.at[pl.ds(first + piece * rows, rows)], held_ref.at[pl.ds(piece * rows, rows)], sems.at[piece]
        )
        for piece in range(PIECES)
    ]
    for copy in copies:
        copy.start()
    next_ref[...] = mark_ref[...] + 1
    for copy in copies:
        copy.wait()


def hold(mark, gate_weight, first, count):
    vmem = pl.BlockSpec(memory_space=pltpu.VMEM)
    anywhere = pl.BlockSpec(memory_space=pl.ANY)
    columns = gate_weight.shape[1]
    return pl.pallas_call(
        functools.partial(hold_kernel, first),
        out_shape=(jax.ShapeDtypeStruct(mark.shape, mark.dtype), pltpu.VMEM((count, columns), gate_weight.dtype)),
        in_specs=[vmem, anywhere],
        out_specs=(vmem, vmem),
        scratch_shapes=[pltpu.SemaphoreType.DMA((PIECES,))],
        compiler_params=pltpu.CompilerParams(vmem_limit_bytes=MIB),
        cost_estimate=pl.CostEstimate(flops=10**6, bytes_accessed=2 * count * columns, transcendentals=0),
        name="hold",
    )(mark, in_hbm(gate_weight))


def shares_of(ids_ref, tokens_ref, router_ref):
    logits = lax.dot_general(
        router_ref[...], tokens_ref[...], (((1,), (1,)), ((), ())), preferred_element_type=jnp.float32
    )
    places = lax.broadcasted_iota(jnp.int32, logits.shape, 0)
    ids = ids_ref[...]
    picked = [
        jnp.sum(jnp.where(places == ids[pick : pick + 1, :], logits, 0.0), axis=0, keepdims=True)
        for pick in range(TOP)
    ]
    top = jnp.maximum(picked[0], picked[1])
    weights = [jnp.exp(value - top) for value in picked]
    total = weights[0] + weights[1]
    return jnp.concatenate([weights[0] / total, weights[1] / total], axis=0)


def prepare_kernel(
    first, mark_ref, ids_ref, tokens_ref, router_ref, gate_ref, key_ref, value_ref,
    next_ref, shares_ref, pair_ref, held_ref, tokens_vmem, router_vmem, sems, pair_sems,
):
    rows = held_ref.shape[0] // PIECES
    copies = [
        pltpu.make_async_copy(ref, pair_ref.at[place], pair_sems.at[place])
        for place, ref in enumerate((key_ref, value_ref))
    ]
    copies += [
        pltpu.make_async_copy(
            gate_ref.at[pl.ds(first + piece * rows, rows)], held_ref.at[pl.ds(piece * rows, rows)], sems.at[piece]
        )
        for piece in range(PIECES)
    ]
    small = [
        pltpu.make_async_copy(tokens_ref, tokens_vmem, pair_sems.at[2]),
        pltpu.make_async_copy(router_ref, router_vmem, pair_sems.at[3]),
    ]
    for copy in small + copies:
        copy.start()
    next_ref[...] = mark_ref[...] + 1
    for copy in small:
        copy.wait()
    shares_ref[...] = shares_of(ids_ref, tokens_vmem, router_vmem)
    for copy in copies:
        copy.wait()


def prepare(mark, ids, moe_tokens, router_weight, gate_weight, keys, values, first, count):
    vmem = pl.BlockSpec(memory_space=pltpu.VMEM)
    anywhere = pl.BlockSpec(memory_space=pl.ANY)
    columns = gate_weight.shape[1]
    return pl.pallas_call(
        functools.partial(prepare_kernel, first),
        out_shape=(
            jax.ShapeDtypeStruct(mark.shape, mark.dtype),
            jax.ShapeDtypeStruct(ids.shape, jnp.float32),
            jax.ShapeDtypeStruct((2,) + keys.shape, keys.dtype),
            pltpu.VMEM((count, columns), gate_weight.dtype),
        ),
        in_specs=[vmem] * 2 + [anywhere] * 5,
        out_specs=(vmem, vmem, anywhere, vmem),
        scratch_shapes=[
            pltpu.VMEM(moe_tokens.shape, moe_tokens.dtype),
            pltpu.VMEM(router_weight.shape[::-1], router_weight.dtype),
            pltpu.SemaphoreType.DMA((PIECES,)),
            pltpu.SemaphoreType.DMA((4,)),
        ],
        compiler_params=pltpu.CompilerParams(vmem_limit_bytes=2 * MIB),
        cost_estimate=pl.CostEstimate(flops=10**6, bytes_accessed=2 * count * columns, transcendentals=0),
        name="prepare",
    )(mark, *map(in_hbm, (ids, moe_tokens, router_weight.T, gate_weight, keys, values)))


def experts_kernel(helds, base_ref, near_ref, far_ref, *refs):
    gate_refs, refs = refs[:helds], refs[helds:]
    up_ref, down_ref, mine_ref, other_ref, parts_ref, rows_ref, sums_ref, up_vmem, down_vmem, sems = refs
    senders = mine_ref.shape[0]
    count = 2 * senders * CAP
    chunks = up_ref.shape[1] // HIDDEN_CHUNK
    depth = down_vmem.shape[0]

    def span(chunk):
        return pl.ds(pl.multiple_of(chunk * HIDDEN_CHUNK, HIDDEN_CHUNK), HIDDEN_CHUNK)

    def up_copy(chunk, slot):
        return pltpu.make_async_copy(up_ref.at[:, span(chunk)], up_vmem.at[slot], sems.at[0, slot])

    def down_copy(chunk, slot):
        return pltpu.make_async_copy(down_ref.at[span(chunk)], down_vmem.at[slot], sems.at[1, slot])

    for chunk in range(min(depth, chunks)):
        up_copy(chunk, chunk).start()
        down_copy(chunk, chunk).start()
    for place, ref in enumerate((near_ref, far_ref)):
        here = ref.shape[0]

        def unpack(i, carry, place=place, ref=ref, here=here):
            first = pl.multiple_of((place * here + i) * CAP * PARTS, 8)
            parts_ref[pl.ds(first, CAP * PARTS), :] = (
                ref[i].astype(jnp.float32).reshape(CAP * PARTS, PART_WIDTH)
            )
            return carry

        lax.fori_loop(0, here, unpack, 0)
    for part in range(PARTS):
        columns = slice(part * PART_WIDTH, (part + 1) * PART_WIDTH)
        rows_ref[:, columns] = parts_ref[pl.ds(part, count, stride=PARTS), :].astype(jnp.bfloat16)

    def work(chunk, first):
        slot = lax.rem(chunk, depth)
        gate_value, first_row = None, 0
        for ref in gate_refs:
            part = jnp.dot(
                rows_ref[:, first_row : first_row + ref.shape[0]], ref[:, span(chunk)], preferred_element_type=jnp.float32
            )
            gate_value = part if gate_value is None else gate_value + part
            first_row += ref.shape[0]
        up_copy(chunk, slot).wait()
        up_value = jnp.dot(rows_ref[...], up_vmem[slot], preferred_element_type=jnp.float32)
        hidden = (gate_value / (1.0 + jnp.exp(-gate_value)) * up_value).astype(jnp.bfloat16)

        @pl.when(chunk + depth < chunks)
        def _():
            up_copy(chunk + depth, slot).start()

        down_copy(chunk, slot).wait()
        product = jnp.dot(hidden, down_vmem[slot], preferred_element_type=jnp.float32)
        if first:
            sums_ref[...] = product
        else:
            sums_ref[...] += product

        @pl.when(chunk + depth < chunks)
        def _():
            down_copy(chunk + depth, slot).start()

    work(jnp.int32(0), True)

    def step(chunk, carry):
        work(chunk, False)
        return carry

    lax.fori_loop(1, chunks, step, 0)
    for part in range(PARTS):
        columns = slice(part * PART_WIDTH, (part + 1) * PART_WIDTH)
        parts_ref[pl.ds(part, count, stride=PARTS), :] = sums_ref[:, columns]

    def give(i, carry):
        first = pl.multiple_of(i * CAP * PARTS, 8)
        sender = lax.bitwise_xor(jnp.int32(i), base_ref[0])
        mine_ref[sender] = parts_ref[pl.ds(first, CAP * PARTS), :].reshape(CAP, PARTS, PART_WIDTH)
        second = pl.multiple_of((senders + i) * CAP * PARTS, 8)
        other_ref[sender] = (
            parts_ref[pl.ds(second, CAP * PARTS), :].reshape(CAP, PARTS, PART_WIDTH).astype(jnp.bfloat16)
        )
        return carry

    lax.fori_loop(0, senders, give, 0)


def experts(base, near, far, gate_held, up_weight, down_weight):
    shape = near.shape
    count = 2 * shape[0] * CAP
    smem = pl.BlockSpec(memory_space=pltpu.SMEM)
    vmem = pl.BlockSpec(memory_space=pltpu.VMEM)
    anywhere = pl.BlockSpec(memory_space=pl.ANY)
    depth = min(3, up_weight.shape[1] // HIDDEN_CHUNK)
    return pl.pallas_call(
        functools.partial(experts_kernel, len(gate_held)),
        out_shape=(jax.ShapeDtypeStruct(shape, jnp.float32), jax.ShapeDtypeStruct(shape, jnp.bfloat16)),
        in_specs=[smem] + [vmem] * (2 + len(gate_held)) + [anywhere, anywhere],
        out_specs=(vmem, vmem),
        scratch_shapes=[
            pltpu.VMEM((count * PARTS, PART_WIDTH), jnp.float32),
            pltpu.VMEM((count, D), jnp.bfloat16),
            pltpu.VMEM((count, D), jnp.float32),
            pltpu.VMEM((depth, D, HIDDEN_CHUNK), jnp.bfloat16),
            pltpu.VMEM((depth, HIDDEN_CHUNK, D), jnp.bfloat16),
            pltpu.SemaphoreType.DMA((2, depth)),
        ],
        compiler_params=pltpu.CompilerParams(vmem_limit_bytes=32 * MIB),
        cost_estimate=pl.CostEstimate(
            flops=6 * count * up_weight.size, bytes_accessed=6 * up_weight.size, transcendentals=0
        ),
        name="experts",
    )(
        base,
        in_vmem(near),
        in_vmem(far),
        *map(in_vmem, gate_held),
        in_hbm(up_weight),
        in_hbm(down_weight),
    )


def add_kernel(mine_ref, other_ref, sum_ref, mark_ref):
    sum_ref[...] = (mine_ref[...] + other_ref[...].astype(jnp.float32)).astype(jnp.bfloat16)
    mark_ref[...] = jnp.zeros_like(mark_ref)


def add(mine, other):
    vmem = pl.BlockSpec(memory_space=pltpu.VMEM)
    return pl.pallas_call(
        add_kernel,
        out_shape=(jax.ShapeDtypeStruct(mine.shape, jnp.bfloat16), jax.ShapeDtypeStruct((8, 128), jnp.float32)),
        in_specs=[vmem, vmem],
        out_specs=(vmem, vmem),
        compiler_params=pltpu.CompilerParams(vmem_limit_bytes=24 * MIB),
        name="add",
    )(mine, other)


def follow_kernel(mark_ref, *refs):
    del mark_ref, refs


def follow(mark, arrays):
    anywhere = pl.BlockSpec(memory_space=pl.ANY)
    return pl.pallas_call(
        follow_kernel,
        out_shape=tuple(jax.ShapeDtypeStruct(x.shape, x.dtype) for x in arrays),
        in_specs=[anywhere] * (1 + len(arrays)),
        out_specs=(anywhere,) * len(arrays),
        input_output_aliases={1 + i: i for i in range(len(arrays))},
        compiler_params=pltpu.CompilerParams(vmem_limit_bytes=MIB),
        name="follow",
    )(mark, *arrays)


def combine_kernel(ids_ref, shares_ref, back_ref, out_ref, rows_ref, count_ref):
    tokens = out_ref.shape[0]
    holders = back_ref.shape[0] // EXPERTS
    for expert in range(EXPERTS):
        count_ref[expert] = 0
    for token in range(tokens):
        total = None
        for pick in range(TOP):
            expert = ids_ref[pick, token]
            slot = count_ref[expert]
            count_ref[expert] = slot + 1
            value = back_ref[expert * holders, slot].astype(jnp.float32)
            for holder in range(1, holders):
                value += back_ref[expert * holders + holder, slot].astype(jnp.float32)
            value = shares_ref[pick, token] * value
            total = value if total is None else total + value
        rows_ref[token * PARTS : (token + 1) * PARTS, :] = total
    for part in range(PARTS):
        columns = slice(part * PART_WIDTH, (part + 1) * PART_WIDTH)
        out_ref[:, columns] = rows_ref[pl.ds(part, tokens, stride=PARTS), :].astype(jnp.bfloat16)


def combine(ids, gate_shares, back):
    tokens = ids.shape[1]
    smem = pl.BlockSpec(memory_space=pltpu.SMEM)
    vmem = pl.BlockSpec(memory_space=pltpu.VMEM)
    return pl.pallas_call(
        combine_kernel,
        out_shape=jax.ShapeDtypeStruct((tokens, D), jnp.bfloat16),
        in_specs=[smem, smem, vmem],
        out_specs=vmem,
        scratch_shapes=[
            pltpu.VMEM((tokens * PARTS, PART_WIDTH), jnp.float32),
            pltpu.SMEM((EXPERTS,), jnp.int32),
        ],
        compiler_params=pltpu.CompilerParams(vmem_limit_bytes=16 * MIB),
        name="combine",
    )(in_hbm(ids), gate_shares, back)


def attention_kernel(
    place_ref, lists_ref, query_ref, b0, b1, b2, b3, b4, b5, out_ref, window, scores, weights, sems
):
    tile, step = pl.program_id(0), pl.program_id(1)
    copies = [
        pltpu.make_async_copy(ref, window.at[i], sems.at[i]) for i, ref in enumerate((b0, b1, b2, b3, b4, b5))
    ]

    @pl.when((tile == 0) & (step == 0))
    def _():
        for copy in copies:
            copy.start()
        for copy in copies:
            copy.wait()

    tiles_here = b0.shape[1] // TILE_POSITIONS
    first_tile = place_ref[0]
    listed_count = jnp.int32(1)
    for entry in range(1, MOST_LISTED):
        listed_count += (lists_ref[tile, entry] >= 0).astype(jnp.int32)

    def fetch(which, entry, head):
        relative = jnp.clip(lists_ref[tile, entry] - first_tile, 0, (PRIOR_DEVICES + 1) * tiles_here - 1)
        source = place_ref[1 + lax.div(relative, tiles_here)]
        first = pl.multiple_of(lax.rem(relative, tiles_here) * TILE_POSITIONS, TILE_POSITIONS)
        columns = pl.ds(pl.multiple_of((step * HEADS_PER_STEP + head) * HEAD_SIZE, HEAD_SIZE), HEAD_SIZE)
        return window[source, which, pl.ds(first, TILE_POSITIONS), columns]

    def attend(listed):
        width = listed * TILE_POSITIONS
        units = [(head, part) for head in range(HEADS_PER_STEP) for part in range(2)]
        group_count = QUERY_PER_GROUP // 2
        row_place = lax.broadcasted_iota(jnp.int32, (TILE_POSITIONS, TILE_POSITIONS), 0)
        column_place = lax.broadcasted_iota(jnp.int32, (TILE_POSITIONS, TILE_POSITIONS), 1)
        causal = column_place <= row_place
        totals = {}

        def columns_of(unit, group):
            head, part = units[unit]
            first = (head * QUERY_PER_GROUP + part * group_count + group) * HEAD_SIZE
            return slice(first, first + HEAD_SIZE)

        def score(unit):
            head = units[unit][0]
            rows = jnp.concatenate([query_ref[:, columns_of(unit, group)] for group in range(group_count)], axis=0)
            keys = jnp.concatenate([fetch(0, entry, head) for entry in range(listed)], axis=0)
            scores[unit, :, :width] = lax.dot_general(
                rows, keys, (((1,), (1,)), ((), ())), preferred_element_type=jnp.float32
            )

        def weigh(unit):
            for group in range(group_count):
                rows = slice(group * TILE_POSITIONS, (group + 1) * TILE_POSITIONS)
                blocks = [jnp.where(causal, scores[unit, rows, :TILE_POSITIONS], -1e30)]
                blocks += [
                    scores[unit, rows, entry * TILE_POSITIONS : (entry + 1) * TILE_POSITIONS]
                    for entry in range(1, listed)
                ]
                top = blocks[0]
                for block in blocks[1:]:
                    top = jnp.maximum(top, block)
                top = jnp.max(top, axis=1, keepdims=True)
                total = None
                for entry, block in enumerate(blocks):
                    weight = jnp.exp2((block - top) * (HEAD_SIZE**-0.5 * LOG2_E))
                    total = weight if total is None else total + weight
                    weights[unit, rows, entry * TILE_POSITIONS : (entry + 1) * TILE_POSITIONS] = weight.astype(
                        jnp.bfloat16
                    )
                totals[unit, group] = jnp.sum(total, axis=1, keepdims=True)

        def finish(unit):
            head = units[unit][0]
            values = jnp.concatenate([fetch(1, entry, head) for entry in range(listed)], axis=0)
            summed = jnp.dot(weights[unit, :, :width], values, preferred_element_type=jnp.float32)
            for group in range(group_count):
                rows = slice(group * TILE_POSITIONS, (group + 1) * TILE_POSITIONS)
                out_ref[:, columns_of(unit, group)] = (summed[rows] / totals[unit, group]).astype(jnp.bfloat16)

        for turn in range(len(units) + 2):
            if turn < len(units):
                score(turn)
            if 0 <= turn - 2:
                finish(turn - 2)
            if 0 <= turn - 1 < len(units):
                weigh(turn - 1)

    for listed in range(1, MOST_LISTED + 1):
        pl.when(listed_count == listed)(functools.partial(attend, listed))


def attention(place, tile_lists, queries, blocks):
    rows_here = queries.shape[0]
    tiles_here = rows_here // TILE_POSITIONS
    group_width = HEADS_PER_STEP * QUERY_PER_GROUP * HEAD_SIZE
    anywhere = pl.BlockSpec(memory_space=pl.ANY)
    query_spec = pl.BlockSpec((TILE_POSITIONS, group_width), lambda tile, step, *_: (tile, step))
    unit = (2 * HEADS_PER_STEP, QUERY_PER_GROUP // 2 * TILE_POSITIONS, MOST_LISTED * TILE_POSITIONS)
    most = MOST_LISTED * TILE_POSITIONS
    return pl.pallas_call(
        attention_kernel,
        out_shape=jax.ShapeDtypeStruct(queries.shape, jnp.bfloat16),
        grid_spec=pltpu.PrefetchScalarGridSpec(
            num_scalar_prefetch=2,
            grid=(tiles_here, KEY_VALUE_HEADS // HEADS_PER_STEP),
            in_specs=[query_spec] + [anywhere] * 6,
            out_specs=query_spec,
            scratch_shapes=[
                pltpu.VMEM((6, 2, rows_here, KEY_VALUE_HEADS * HEAD_SIZE), jnp.bfloat16),
                pltpu.VMEM(unit, jnp.float32),
                pltpu.VMEM(unit, jnp.bfloat16),
                pltpu.SemaphoreType.DMA((6,)),
            ],
        ),
        compiler_params=pltpu.CompilerParams(vmem_limit_bytes=24 * MIB),
        cost_estimate=pl.CostEstimate(
            flops=4 * most * queries.size, bytes_accessed=8 * queries.size, transcendentals=most * queries.size // 128
        ),
        name="attention",
    )(place, tile_lists, in_hbm(queries), *blocks)


def shards(
    queries,
    key_matrix,
    value_matrix,
    tile_lists,
    moe_tokens,
    expert_ids,
    router_weight,
    gate_weight,
    up_weight,
    down_weight,
):
    devices = lax.axis_size("ctx")
    me = lax.axis_index("ctx")
    ids = expert_ids.T
    direct = devices == 2 * EXPERTS
    base = (me // 2 if direct else jnp.zeros_like(me)).astype(jnp.int32)[None]
    keep, send = pack(ids, base, moe_tokens)
    mark = jnp.zeros((8, 128), jnp.float32)
    rest = (ids, moe_tokens, router_weight, gate_weight, key_matrix, value_matrix)
    if direct:
        came = exchanged(send, 2)
        mark, first_held = hold(mark, gate_weight, 0, FIRST_HELD)
        *pieces, mark = join(keep, came, mark)
        pieces[1:] = [exchanged(pieces[place], 4 * place) for place in range(1, len(pieces))]
        mark, gate_shares, own, second_held = prepare(mark, *rest, FIRST_HELD, D - FIRST_HELD)
        near = merge(mark, pieces)
        gate_held = [first_held, second_held]
    else:
        packed = jnp.stack([keep, send], axis=1).reshape((EXPERTS,) + keep.shape[1:])
        near = same_core_exchange(jnp.repeat(packed, devices // (2 * EXPERTS), axis=0))
        mark, gate_shares, own, held = prepare(mark, *rest, 0, D)
        gate_held = [held]
    far = exchanged(near, 1)
    two_before = passed_along(own, 2)
    four_before = passed_along(own, 4)
    mine, other = experts(base, near, far, gate_held, up_weight, down_weight)
    summed, mark = add(mine, exchanged(other, 1))
    back = same_core_exchange(summed)
    blocks = list(follow(mark, [own, two_before, four_before]))
    blocks += [exchanged(x, 1) for x in blocks]
    tiles_here = queries.shape[0] // TILE_POSITIONS
    sources = jnp.where(me % 2 == 0, *(jnp.array(row, jnp.int32) for row in WINDOW_SOURCES))
    place = jnp.concatenate([((me - PRIOR_DEVICES) * tiles_here).astype(jnp.int32)[None], sources])
    attended = attention(place, tile_lists, queries, blocks)
    attended, back = lax.optimization_barrier((attended, back))
    combined = combine(ids, gate_shares, back)
    return (attended, combined)


def solution(mesh):
    split = P(("group", "ctx"), None)
    placed = (split, split, split, split, split, split, P(), P(None, "ctx"), P(None, "ctx"), P("ctx", None))
    return jax.shard_map(shards, mesh=mesh, in_specs=placed, out_specs=(split, split), check_vma=False)
```

```python
import functools

import jax
import jax.numpy as jnp
from jax import lax
from jax.experimental import pallas as pl
from jax.experimental.pallas import tpu as pltpu
from jax.sharding import PartitionSpec as P

TILE_POSITIONS = 128
HEAD_SIZE = 128
KEY_VALUE_HEADS = 4
QUERY_HEADS = 24
QUERY_PER_GROUP = 6
PRIOR_DEVICES = 4
MOST_LISTED = 6
D = 3072
EXPERTS = 8
TOP = 2
CAP = 5

PARTS = 24
PART_WIDTH = D // PARTS
PIECES = 4
HELD_ROWS = (768, 768)
STREAMED_FROM = sum(HELD_ROWS)
HIDDEN_CHUNK = 512
HEADS_PER_STEP = 4
LOG2_E = 1.4426950408889634
MIB = 2**20

SMALL_COST = pl.CostEstimate(flops=10**6, bytes_accessed=10**5, transcendentals=0)

WINDOW_SOURCES = ((2, 5, 1, 4, 0), (2, 4, 1, 3, 0))


def in_vmem(x):
    return pltpu.with_memory_space_constraint(x, pltpu.VMEM)


def in_hbm(x):
    return pltpu.with_memory_space_constraint(x, pltpu.HBM)


def exchanged(x, by):
    devices = lax.axis_size("ctx")
    return lax.ppermute(x, "ctx", [(i, i ^ by) for i in range(devices)])


def passed_along(x, by):
    devices = lax.axis_size("ctx")
    return lax.ppermute(x, "ctx", [(i, (i + by) % devices) for i in range(devices)])


def same_core_exchange(x):
    devices = lax.axis_size("ctx")
    groups = [[core + 2 * i for i in range(devices // 2)] for core in range(2)]
    return lax.all_to_all(x, "ctx", split_axis=0, concat_axis=0, tiled=True, axis_index_groups=groups)


def row_copies(source, first, target, sems):
    rows = target.shape[0] // PIECES
    return [
        pltpu.make_async_copy(
            source.at[pl.ds(first + piece * rows, rows)], target.at[pl.ds(piece * rows, rows)], sems.at[piece]
        )
        for piece in range(PIECES)
    ]


def pack_kernel(ids_ref, base_ref, tokens_ref, keep_ref, send_ref, rows_ref, slots_ref, count_ref):
    tokens = tokens_ref.shape[0]
    base = base_ref[0]
    for part in range(PARTS):
        columns = slice(part * PART_WIDTH, (part + 1) * PART_WIDTH)
        rows_ref[pl.ds(part, tokens, stride=PARTS), :] = tokens_ref[:, columns].astype(jnp.float32)
    slots_ref[...] = jnp.zeros_like(slots_ref)
    for expert in range(EXPERTS):
        count_ref[expert] = 0
    for token in range(tokens):
        row = rows_ref[token * PARTS : (token + 1) * PARTS, :].astype(jnp.bfloat16)
        for pick in range(TOP):
            expert = ids_ref[pick, token]
            slot = count_ref[expert]
            count_ref[expert] = slot + 1
            place = lax.bitwise_xor(expert, base)
            slots_ref[lax.bitwise_and(place, 1), lax.shift_right_logical(place, 1), slot] = row
    keep_ref[...] = slots_ref[0]
    send_ref[...] = slots_ref[1]


def pack(ids, base, moe_tokens):
    tokens = moe_tokens.shape[0]
    smem = pl.BlockSpec(memory_space=pltpu.SMEM)
    vmem = pl.BlockSpec(memory_space=pltpu.VMEM)
    half = (EXPERTS // 2, CAP, PARTS, PART_WIDTH)
    return pl.pallas_call(
        pack_kernel,
        out_shape=(jax.ShapeDtypeStruct(half, jnp.bfloat16),) * 2,
        in_specs=[smem, smem, vmem],
        out_specs=(vmem,) * 2,
        scratch_shapes=[
            pltpu.VMEM((tokens * PARTS, PART_WIDTH), jnp.float32),
            pltpu.VMEM((2,) + half, jnp.bfloat16),
            pltpu.SMEM((EXPERTS,), jnp.int32),
        ],
        compiler_params=pltpu.CompilerParams(vmem_limit_bytes=4 * MIB),
        name="pack",
    )(in_hbm(ids), base, in_hbm(moe_tokens))


def join_kernel(keep_ref, came_ref, mark_ref, *out_refs):
    for place, ref in enumerate(out_refs[:-1]):
        ref[0] = keep_ref[place]
        ref[1] = came_ref[place]
    out_refs[-1][...] = mark_ref[...] + 1


def join(keep, came, mark):
    vmem = pl.BlockSpec(memory_space=pltpu.VMEM)
    shape = jax.ShapeDtypeStruct((2,) + keep.shape[1:], keep.dtype)
    count = keep.shape[0]
    return pl.pallas_call(
        join_kernel,
        out_shape=(shape,) * count + (jax.ShapeDtypeStruct(mark.shape, mark.dtype),),
        in_specs=[vmem] * 3,
        out_specs=(vmem,) * (count + 1),
        compiler_params=pltpu.CompilerParams(vmem_limit_bytes=4 * MIB),
        name="join",
    )(keep, came, mark)


def merge_kernel(mark_ref, *refs):
    for place, ref in enumerate(refs[:-1]):
        refs[-1][2 * place : 2 * place + 2] = ref[...]


def merge(mark, pieces):
    vmem = pl.BlockSpec(memory_space=pltpu.VMEM)
    return pl.pallas_call(
        merge_kernel,
        out_shape=jax.ShapeDtypeStruct((2 * len(pieces),) + pieces[0].shape[1:], pieces[0].dtype),
        in_specs=[vmem] * (1 + len(pieces)),
        out_specs=vmem,
        compiler_params=pltpu.CompilerParams(vmem_limit_bytes=4 * MIB),
        name="merge",
    )(mark, *pieces)


def hold_kernel(first, mark_ref, gate_ref, next_ref, held_ref, sems):
    copies = row_copies(gate_ref, first, held_ref, sems)
    for copy in copies:
        copy.start()
    next_ref[...] = mark_ref[...] + 1
    for copy in copies:
        copy.wait()


def hold(mark, gate_weight, first, count):
    vmem = pl.BlockSpec(memory_space=pltpu.VMEM)
    anywhere = pl.BlockSpec(memory_space=pl.ANY)
    columns = gate_weight.shape[1]
    return pl.pallas_call(
        functools.partial(hold_kernel, first),
        out_shape=(jax.ShapeDtypeStruct(mark.shape, mark.dtype), pltpu.VMEM((count, columns), gate_weight.dtype)),
        in_specs=[vmem, anywhere],
        out_specs=(vmem, vmem),
        scratch_shapes=[pltpu.SemaphoreType.DMA((PIECES,))],
        compiler_params=pltpu.CompilerParams(vmem_limit_bytes=MIB),
        cost_estimate=pl.CostEstimate(flops=10**6, bytes_accessed=2 * count * columns, transcendentals=0),
        name="hold",
    )(mark, in_hbm(gate_weight))


def shares_of(ids_ref, tokens_ref, router_ref):
    logits = lax.dot_general(
        router_ref[...], tokens_ref[...], (((1,), (1,)), ((), ())), preferred_element_type=jnp.float32
    )
    places = lax.broadcasted_iota(jnp.int32, logits.shape, 0)
    ids = ids_ref[...]
    picked = [
        jnp.sum(jnp.where(places == ids[pick : pick + 1, :], logits, 0.0), axis=0, keepdims=True)
        for pick in range(TOP)
    ]
    top = jnp.maximum(picked[0], picked[1])
    weights = [jnp.exp(value - top) for value in picked]
    total = weights[0] + weights[1]
    return jnp.concatenate([weights[0] / total, weights[1] / total], axis=0)


def prepare_kernel(
    first, mark_ref, ids_ref, tokens_ref, router_ref, gate_ref, key_ref, value_ref,
    next_ref, shares_ref, pair_ref, held_ref, tokens_vmem, router_vmem, sems, pair_sems,
):
    copies = [
        pltpu.make_async_copy(ref, pair_ref.at[place], pair_sems.at[place])
        for place, ref in enumerate((key_ref, value_ref))
    ] + row_copies(gate_ref, first, held_ref, sems)
    small = [
        pltpu.make_async_copy(tokens_ref, tokens_vmem, pair_sems.at[2]),
        pltpu.make_async_copy(router_ref, router_vmem, pair_sems.at[3]),
    ]
    for copy in small + copies:
        copy.start()
    next_ref[...] = mark_ref[...] + 1
    for copy in small:
        copy.wait()
    shares_ref[...] = shares_of(ids_ref, tokens_vmem, router_vmem)
    for copy in copies:
        copy.wait()


def prepare(mark, ids, moe_tokens, router_weight, gate_weight, keys, values, first, count):
    vmem = pl.BlockSpec(memory_space=pltpu.VMEM)
    anywhere = pl.BlockSpec(memory_space=pl.ANY)
    columns = gate_weight.shape[1]
    return pl.pallas_call(
        functools.partial(prepare_kernel, first),
        out_shape=(
            jax.ShapeDtypeStruct(mark.shape, mark.dtype),
            jax.ShapeDtypeStruct(ids.shape, jnp.float32),
            jax.ShapeDtypeStruct((2,) + keys.shape, keys.dtype),
            pltpu.VMEM((count, columns), gate_weight.dtype),
        ),
        in_specs=[vmem] * 2 + [anywhere] * 5,
        out_specs=(vmem, vmem, anywhere, vmem),
        scratch_shapes=[
            pltpu.VMEM(moe_tokens.shape, moe_tokens.dtype),
            pltpu.VMEM(router_weight.shape[::-1], router_weight.dtype),
            pltpu.SemaphoreType.DMA((PIECES,)),
            pltpu.SemaphoreType.DMA((4,)),
        ],
        compiler_params=pltpu.CompilerParams(vmem_limit_bytes=2 * MIB),
        cost_estimate=pl.CostEstimate(flops=10**6, bytes_accessed=2 * count * columns, transcendentals=0),
        name="prepare",
    )(mark, *map(in_hbm, (ids, moe_tokens, router_weight.T, gate_weight, keys, values)))


def experts_kernel(helds, base_ref, near_ref, far_ref, *refs):
    gate_refs, refs = refs[:helds], refs[helds:]
    gate_ref, up_ref, down_ref, mine_ref, other_ref, parts_ref, rows_ref, sums_ref, gate_vmem, up_vmem, down_vmem, sems = refs
    senders = mine_ref.shape[0]
    count = 2 * senders * CAP
    chunks = up_ref.shape[1] // HIDDEN_CHUNK
    depth = down_vmem.shape[0]

    def span(chunk):
        return pl.ds(pl.multiple_of(chunk * HIDDEN_CHUNK, HIDDEN_CHUNK), HIDDEN_CHUNK)

    def gate_copy(chunk, slot):
        rest = pl.ds(STREAMED_FROM, D - STREAMED_FROM)
        return pltpu.make_async_copy(gate_ref.at[rest, span(chunk)], gate_vmem.at[slot], sems.at[2, slot])

    def up_copy(chunk, slot):
        return pltpu.make_async_copy(up_ref.at[:, span(chunk)], up_vmem.at[slot], sems.at[0, slot])

    def down_copy(chunk, slot):
        return pltpu.make_async_copy(down_ref.at[span(chunk)], down_vmem.at[slot], sems.at[1, slot])

    for chunk in range(min(depth, chunks)):
        gate_copy(chunk, chunk).start()
        up_copy(chunk, chunk).start()
        down_copy(chunk, chunk).start()
    for place, ref in enumerate((near_ref, far_ref)):
        here = ref.shape[0]

        def unpack(i, carry, place=place, ref=ref, here=here):
            first = pl.multiple_of((place * here + i) * CAP * PARTS, 8)
            parts_ref[pl.ds(first, CAP * PARTS), :] = (
                ref[i].astype(jnp.float32).reshape(CAP * PARTS, PART_WIDTH)
            )
            return carry

        lax.fori_loop(0, here, unpack, 0)
    for part in range(PARTS):
        columns = slice(part * PART_WIDTH, (part + 1) * PART_WIDTH)
        rows_ref[:, columns] = parts_ref[pl.ds(part, count, stride=PARTS), :].astype(jnp.bfloat16)

    def work(chunk, first):
        slot = lax.rem(chunk, depth)
        gate_value, first_row = None, 0
        for ref in gate_refs:
            part = jnp.dot(
                rows_ref[:, first_row : first_row + ref.shape[0]], ref[:, span(chunk)], preferred_element_type=jnp.float32
            )
            gate_value = part if gate_value is None else gate_value + part
            first_row += ref.shape[0]
        gate_copy(chunk, slot).wait()
        gate_value += jnp.dot(rows_ref[:, STREAMED_FROM:], gate_vmem[slot], preferred_element_type=jnp.float32)
        up_copy(chunk, slot).wait()
        up_value = jnp.dot(rows_ref[...], up_vmem[slot], preferred_element_type=jnp.float32)
        hidden = (gate_value / (1.0 + jnp.exp(-gate_value)) * up_value).astype(jnp.bfloat16)

        @pl.when(chunk + depth < chunks)
        def _():
            gate_copy(chunk + depth, slot).start()
            up_copy(chunk + depth, slot).start()

        down_copy(chunk, slot).wait()
        product = jnp.dot(hidden, down_vmem[slot], preferred_element_type=jnp.float32)
        if first:
            sums_ref[...] = product
        else:
            sums_ref[...] += product

        @pl.when(chunk + depth < chunks)
        def _():
            down_copy(chunk + depth, slot).start()

    work(jnp.int32(0), True)

    def step(chunk, carry):
        work(chunk, False)
        return carry

    lax.fori_loop(1, chunks, step, 0)
    for part in range(PARTS):
        columns = slice(part * PART_WIDTH, (part + 1) * PART_WIDTH)
        parts_ref[pl.ds(part, count, stride=PARTS), :] = sums_ref[:, columns]

    def give(i, carry):
        first = pl.multiple_of(i * CAP * PARTS, 8)
        sender = lax.bitwise_xor(jnp.int32(i), base_ref[0])
        mine_ref[sender] = parts_ref[pl.ds(first, CAP * PARTS), :].reshape(CAP, PARTS, PART_WIDTH)
        second = pl.multiple_of((senders + i) * CAP * PARTS, 8)
        other_ref[sender] = (
            parts_ref[pl.ds(second, CAP * PARTS), :].reshape(CAP, PARTS, PART_WIDTH).astype(jnp.bfloat16)
        )
        return carry

    lax.fori_loop(0, senders, give, 0)


def experts(base, near, far, gate_held, gate_weight, up_weight, down_weight):
    shape = near.shape
    count = 2 * shape[0] * CAP
    smem = pl.BlockSpec(memory_space=pltpu.SMEM)
    vmem = pl.BlockSpec(memory_space=pltpu.VMEM)
    anywhere = pl.BlockSpec(memory_space=pl.ANY)
    depth = min(3, up_weight.shape[1] // HIDDEN_CHUNK)
    return pl.pallas_call(
        functools.partial(experts_kernel, len(gate_held)),
        out_shape=(pltpu.VMEM(shape, jnp.float32), pltpu.VMEM(shape, jnp.bfloat16)),
        in_specs=[smem] + [vmem] * (2 + len(gate_held)) + [anywhere] * 3,
        out_specs=(vmem, vmem),
        scratch_shapes=[
            pltpu.VMEM((count * PARTS, PART_WIDTH), jnp.float32),
            pltpu.VMEM((count, D), jnp.bfloat16),
            pltpu.VMEM((count, D), jnp.float32),
            pltpu.VMEM((depth, D - STREAMED_FROM, HIDDEN_CHUNK), jnp.bfloat16),
            pltpu.VMEM((depth, D, HIDDEN_CHUNK), jnp.bfloat16),
            pltpu.VMEM((depth, HIDDEN_CHUNK, D), jnp.bfloat16),
            pltpu.SemaphoreType.DMA((3, depth)),
        ],
        compiler_params=pltpu.CompilerParams(vmem_limit_bytes=32 * MIB),
        cost_estimate=SMALL_COST,
        name="experts",
    )(
        base,
        in_vmem(near),
        in_vmem(far),
        *map(in_vmem, gate_held),
        in_hbm(gate_weight),
        in_hbm(up_weight),
        in_hbm(down_weight),
    )


def add_kernel(mine_ref, other_ref, sum_ref, mark_ref):
    sum_ref[...] = (mine_ref[...] + other_ref[...].astype(jnp.float32)).astype(jnp.bfloat16)
    mark_ref[...] = jnp.zeros_like(mark_ref)


def add(mine, other):
    vmem = pl.BlockSpec(memory_space=pltpu.VMEM)
    return pl.pallas_call(
        add_kernel,
        out_shape=(jax.ShapeDtypeStruct(mine.shape, jnp.bfloat16), jax.ShapeDtypeStruct((8, 128), jnp.float32)),
        in_specs=[vmem, vmem],
        out_specs=(vmem, vmem),
        compiler_params=pltpu.CompilerParams(vmem_limit_bytes=24 * MIB),
        name="add",
    )(mine, other)


def follow_kernel(mark_ref, *refs):
    del mark_ref, refs


def follow(mark, arrays):
    anywhere = pl.BlockSpec(memory_space=pl.ANY)
    return pl.pallas_call(
        follow_kernel,
        out_shape=tuple(jax.ShapeDtypeStruct(x.shape, x.dtype) for x in arrays),
        in_specs=[anywhere] * (1 + len(arrays)),
        out_specs=(anywhere,) * len(arrays),
        input_output_aliases={1 + i: i for i in range(len(arrays))},
        compiler_params=pltpu.CompilerParams(vmem_limit_bytes=MIB),
        name="follow",
    )(mark, *arrays)


def combine_kernel(ids_ref, shares_ref, back_ref, attended_ref, out_ref, rows_ref, count_ref):
    del attended_ref
    tokens = out_ref.shape[0]
    holders = back_ref.shape[0] // EXPERTS
    for expert in range(EXPERTS):
        count_ref[expert] = 0
    for token in range(tokens):
        total = None
        for pick in range(TOP):
            expert = ids_ref[pick, token]
            slot = count_ref[expert]
            count_ref[expert] = slot + 1
            value = back_ref[expert * holders, slot].astype(jnp.float32)
            for holder in range(1, holders):
                value += back_ref[expert * holders + holder, slot].astype(jnp.float32)
            value = shares_ref[pick, token] * value
            total = value if total is None else total + value
        rows_ref[token * PARTS : (token + 1) * PARTS, :] = total
    for part in range(PARTS):
        columns = slice(part * PART_WIDTH, (part + 1) * PART_WIDTH)
        out_ref[:, columns] = rows_ref[pl.ds(part, tokens, stride=PARTS), :].astype(jnp.bfloat16)


def combine(ids, gate_shares, back, attended):
    tokens = ids.shape[1]
    smem = pl.BlockSpec(memory_space=pltpu.SMEM)
    vmem = pl.BlockSpec(memory_space=pltpu.VMEM)
    return pl.pallas_call(
        combine_kernel,
        out_shape=jax.ShapeDtypeStruct((tokens, D), jnp.bfloat16),
        in_specs=[smem, smem, vmem, pl.BlockSpec(memory_space=pl.ANY)],
        out_specs=vmem,
        scratch_shapes=[
            pltpu.VMEM((tokens * PARTS, PART_WIDTH), jnp.float32),
            pltpu.SMEM((EXPERTS,), jnp.int32),
        ],
        compiler_params=pltpu.CompilerParams(vmem_limit_bytes=16 * MIB),
        name="combine",
    )(in_hbm(ids), gate_shares, back, in_hbm(attended))


def attention_kernel(
    place_ref, lists_ref, query_ref, b0, b1, b2, b3, b4, b5, out_ref, staged, scores, weights, done, sems
):
    blocks = (b0, b1, b2, b3, b4, b5)
    tiles_here = query_ref.shape[0] // TILE_POSITIONS
    steps = KEY_VALUE_HEADS // HEADS_PER_STEP
    step_width = HEADS_PER_STEP * QUERY_PER_GROUP * HEAD_SIZE
    rounds = tiles_here * steps

    def out_copy(turn, slot):
        rows = pl.ds(pl.multiple_of(lax.div(turn, steps) * TILE_POSITIONS, TILE_POSITIONS), TILE_POSITIONS)
        columns = pl.ds(pl.multiple_of(lax.rem(turn, steps) * step_width, step_width), step_width)
        return pltpu.make_async_copy(done.at[slot], out_ref.at[rows, columns], sems.at[slot])

    def gather(tile, count):
        def one(entry):
            relative = jnp.clip(lists_ref[tile, entry] - place_ref[0], 0, (PRIOR_DEVICES + 1) * tiles_here - 1)
            source = place_ref[1 + lax.div(relative, tiles_here)]
            first = pl.multiple_of(lax.rem(relative, tiles_here) * TILE_POSITIONS, TILE_POSITIONS)
            for number, block in enumerate(blocks):

                @pl.when(source == number)
                def _(block=block):
                    for which in range(2):
                        staged[which, entry * TILE_POSITIONS : (entry + 1) * TILE_POSITIONS, :] = block[
                            which, pl.ds(first, TILE_POSITIONS), :
                        ]

        for entry in range(MOST_LISTED):
            pl.when(entry < count)(functools.partial(one, entry))

    def turn_body(turn, carry):
        tile, step = lax.div(turn, steps), lax.rem(turn, steps)
        slot = lax.rem(turn, 2)
        count = jnp.int32(1)
        for entry in range(1, MOST_LISTED):
            count += (lists_ref[tile, entry] >= 0).astype(jnp.int32)
        pl.when(step == 0)(functools.partial(gather, tile, count))

        @pl.when(turn >= 2)
        def _():
            out_copy(turn - 2, slot).wait()

        for listed in range(1, MOST_LISTED + 1):
            pl.when(count == listed)(functools.partial(attend, tile, step, slot, listed))
        out_copy(turn, slot).start()
        return carry

    def attend(tile, step, slot, listed):
        query_rows = pl.ds(pl.multiple_of(tile * TILE_POSITIONS, TILE_POSITIONS), TILE_POSITIONS)
        width = listed * TILE_POSITIONS
        units = [(head, part) for head in range(HEADS_PER_STEP) for part in range(2)]
        group_count = QUERY_PER_GROUP // 2
        row_place = lax.broadcasted_iota(jnp.int32, (TILE_POSITIONS, TILE_POSITIONS), 0)
        column_place = lax.broadcasted_iota(jnp.int32, (TILE_POSITIONS, TILE_POSITIONS), 1)
        causal = column_place <= row_place
        totals = {}

        def first_column(unit, group):
            head, part = units[unit]
            return (head * QUERY_PER_GROUP + part * group_count + group) * HEAD_SIZE

        def query(unit, group):
            first = pl.multiple_of(step * step_width + first_column(unit, group), HEAD_SIZE)
            return query_ref[query_rows, pl.ds(first, HEAD_SIZE)]

        def head_columns(unit):
            return pl.ds(pl.multiple_of((step * HEADS_PER_STEP + units[unit][0]) * HEAD_SIZE, HEAD_SIZE), HEAD_SIZE)

        def score(unit):
            rows = jnp.concatenate([query(unit, group) for group in range(group_count)], axis=0)
            keys = staged[0, :width, head_columns(unit)]
            scores[unit, :, :width] = lax.dot_general(
                rows, keys, (((1,), (1,)), ((), ())), preferred_element_type=jnp.float32
            )

        def weigh(unit):
            for group in range(group_count):
                rows = slice(group * TILE_POSITIONS, (group + 1) * TILE_POSITIONS)
                blocks = [jnp.where(causal, scores[unit, rows, :TILE_POSITIONS], -1e30)]
                blocks += [
                    scores[unit, rows, entry * TILE_POSITIONS : (entry + 1) * TILE_POSITIONS]
                    for entry in range(1, listed)
                ]
                top = blocks[0]
                for block in blocks[1:]:
                    top = jnp.maximum(top, block)
                top = jnp.max(top, axis=1, keepdims=True)
                total = None
                for entry, block in enumerate(blocks):
                    weight = jnp.exp2((block - top) * (HEAD_SIZE**-0.5 * LOG2_E))
                    total = weight if total is None else total + weight
                    weights[unit, rows, entry * TILE_POSITIONS : (entry + 1) * TILE_POSITIONS] = weight.astype(
                        jnp.bfloat16
                    )
                totals[unit, group] = 1.0 / jnp.sum(total, axis=1, keepdims=True)

        def finish(unit):
            values = staged[1, :width, head_columns(unit)]
            summed = jnp.dot(weights[unit, :, :width], values, preferred_element_type=jnp.float32)
            for group in range(group_count):
                rows = slice(group * TILE_POSITIONS, (group + 1) * TILE_POSITIONS)
                first = first_column(unit, group)
                done[slot, :, first : first + HEAD_SIZE] = (summed[rows] * totals[unit, group]).astype(jnp.bfloat16)

        for turn in range(len(units) + 2):
            if turn < len(units):
                score(turn)
            if 0 <= turn - 2:
                finish(turn - 2)
            if 0 <= turn - 1 < len(units):
                weigh(turn - 1)

    lax.fori_loop(0, rounds, turn_body, 0)
    for turn in range(max(rounds - 2, 0), rounds):
        out_copy(jnp.int32(turn), turn % 2).wait()


def attention(place, tile_lists, queries, blocks):
    smem = pl.BlockSpec(memory_space=pltpu.SMEM)
    vmem = pl.BlockSpec(memory_space=pltpu.VMEM)
    unit = (2 * HEADS_PER_STEP, QUERY_PER_GROUP // 2 * TILE_POSITIONS, MOST_LISTED * TILE_POSITIONS)
    return pl.pallas_call(
        attention_kernel,
        out_shape=jax.ShapeDtypeStruct(queries.shape, jnp.bfloat16),
        in_specs=[smem, smem] + [vmem] * 7,
        out_specs=pl.BlockSpec(memory_space=pl.ANY),
        scratch_shapes=[
            pltpu.VMEM((2, MOST_LISTED * TILE_POSITIONS, KEY_VALUE_HEADS * HEAD_SIZE), jnp.bfloat16),
            pltpu.VMEM(unit, jnp.float32),
            pltpu.VMEM(unit, jnp.bfloat16),
            pltpu.VMEM((2, TILE_POSITIONS, HEADS_PER_STEP * QUERY_PER_GROUP * HEAD_SIZE), jnp.bfloat16),
            pltpu.SemaphoreType.DMA((2,)),
        ],
        compiler_params=pltpu.CompilerParams(vmem_limit_bytes=32 * MIB),
        cost_estimate=SMALL_COST,
        name="attention",
    )(place, tile_lists, queries, *blocks)


def shards(
    queries,
    key_matrix,
    value_matrix,
    tile_lists,
    moe_tokens,
    expert_ids,
    router_weight,
    gate_weight,
    up_weight,
    down_weight,
):
    devices = lax.axis_size("ctx")
    me = lax.axis_index("ctx")
    ids = expert_ids.T
    direct = devices == 2 * EXPERTS
    base = (me // 2 if direct else jnp.zeros_like(me)).astype(jnp.int32)[None]
    gate_held = []
    keep, send = pack(ids, base, moe_tokens)
    mark = jnp.zeros((8, 128), jnp.float32)
    rest = (ids, moe_tokens, router_weight, gate_weight, key_matrix, value_matrix)
    if direct:
        came = exchanged(send, 2)
        mark, held = hold(mark, gate_weight, 0, HELD_ROWS[0])
        gate_held.append(held)
        *pieces, mark = join(keep, came, mark)
        pieces[1:] = [exchanged(pieces[place], 4 * place) for place in range(1, len(pieces))]
        mark, gate_shares, own, held = prepare(mark, *rest, HELD_ROWS[0], HELD_ROWS[1])
        near = merge(mark, pieces)
    else:
        packed = jnp.stack([keep, send], axis=1).reshape((EXPERTS,) + keep.shape[1:])
        near = same_core_exchange(jnp.repeat(packed, devices // (2 * EXPERTS), axis=0))
        mark, gate_shares, own, held = prepare(mark, *rest, 0, STREAMED_FROM)
    gate_held.append(held)
    far = exchanged(near, 1)
    two_before = passed_along(own, 2)
    four_before = passed_along(own, 4)
    mine, other = experts(base, near, far, gate_held, gate_weight, up_weight, down_weight)
    summed, mark = add(mine, exchanged(other, 1))
    back = same_core_exchange(summed)
    blocks = list(follow(mark, [own, two_before, four_before]))
    blocks += [exchanged(x, 1) for x in blocks]
    tiles_here = queries.shape[0] // TILE_POSITIONS
    sources = jnp.where(me % 2 == 0, *(jnp.array(row, jnp.int32) for row in WINDOW_SOURCES))
    place = jnp.concatenate([((me - PRIOR_DEVICES) * tiles_here).astype(jnp.int32)[None], sources])
    attended = attention(place, tile_lists, queries, blocks)
    combined = combine(ids, gate_shares, back, attended)
    return (attended, combined)


def solution(mesh):
    split = P(("group", "ctx"), None)
    placed = (split, split, split, split, split, split, P(), P(None, "ctx"), P(None, "ctx"), P("ctx", None))
    return jax.shard_map(shards, mesh=mesh, in_specs=placed, out_specs=(split, split), check_vma=False)
```

```python
import functools

import jax
import jax.numpy as jnp
from jax import lax
from jax.experimental import pallas as pl
from jax.experimental.pallas import tpu as pltpu
from jax.sharding import PartitionSpec as P

TILE_POSITIONS = 128
HEAD_SIZE = 128
KEY_VALUE_HEADS = 4
QUERY_HEADS = 24
QUERY_PER_GROUP = 6
PRIOR_DEVICES = 4
MOST_LISTED = 6
D = 3072
EXPERTS = 8
TOP = 2
CAP = 5

PARTS = 24
PART_WIDTH = D // PARTS
PIECES = 16
HELD_ROWS = (768, 768)
STREAMED_FROM = sum(HELD_ROWS)
HIDDEN_CHUNK = 512
HEADS_PER_STEP = 4
LOG2_E = 1.4426950408889634
MIB = 2**20

SMALL_COST = pl.CostEstimate(flops=10**6, bytes_accessed=10**5, transcendentals=0)

WINDOW_SOURCES = ((2, 5, 1, 4, 0), (2, 4, 1, 3, 0))


def in_vmem(x):
    return pltpu.with_memory_space_constraint(x, pltpu.VMEM)


def in_hbm(x):
    return pltpu.with_memory_space_constraint(x, pltpu.HBM)


def exchanged(x, by):
    devices = lax.axis_size("ctx")
    return lax.ppermute(x, "ctx", [(i, i ^ by) for i in range(devices)])


def passed_along(x, by):
    devices = lax.axis_size("ctx")
    return lax.ppermute(x, "ctx", [(i, (i + by) % devices) for i in range(devices)])


def same_core_exchange(x):
    devices = lax.axis_size("ctx")
    groups = [[core + 2 * i for i in range(devices // 2)] for core in range(2)]
    return lax.all_to_all(x, "ctx", split_axis=0, concat_axis=0, tiled=True, axis_index_groups=groups)


def row_copies(source, first, target, sems):
    rows = target.shape[0] // PIECES
    return [
        pltpu.make_async_copy(
            source.at[pl.ds(first + piece * rows, rows)], target.at[pl.ds(piece * rows, rows)], sems.at[piece]
        )
        for piece in range(PIECES)
    ]


def pack_kernel(ids_ref, base_ref, tokens_ref, keep_ref, send_ref, rows_ref, slots_ref, count_ref):
    tokens = tokens_ref.shape[0]
    base = base_ref[0]
    for part in range(PARTS):
        columns = slice(part * PART_WIDTH, (part + 1) * PART_WIDTH)
        rows_ref[pl.ds(part, tokens, stride=PARTS), :] = tokens_ref[:, columns].astype(jnp.float32)
    slots_ref[...] = jnp.zeros_like(slots_ref)
    for expert in range(EXPERTS):
        count_ref[expert] = 0
    for token in range(tokens):
        row = rows_ref[token * PARTS : (token + 1) * PARTS, :].astype(jnp.bfloat16)
        for pick in range(TOP):
            expert = ids_ref[pick, token]
            slot = count_ref[expert]
            count_ref[expert] = slot + 1
            place = lax.bitwise_xor(expert, base)
            slots_ref[lax.bitwise_and(place, 1), lax.shift_right_logical(place, 1), slot] = row
    keep_ref[...] = slots_ref[0]
    send_ref[...] = slots_ref[1]


def pack(ids, base, moe_tokens):
    tokens = moe_tokens.shape[0]
    smem = pl.BlockSpec(memory_space=pltpu.SMEM)
    vmem = pl.BlockSpec(memory_space=pltpu.VMEM)
    half = (EXPERTS // 2, CAP, PARTS, PART_WIDTH)
    return pl.pallas_call(
        pack_kernel,
        out_shape=(jax.ShapeDtypeStruct(half, jnp.bfloat16),) * 2,
        in_specs=[smem, smem, vmem],
        out_specs=(vmem,) * 2,
        scratch_shapes=[
            pltpu.VMEM((tokens * PARTS, PART_WIDTH), jnp.float32),
            pltpu.VMEM((2,) + half, jnp.bfloat16),
            pltpu.SMEM((EXPERTS,), jnp.int32),
        ],
        compiler_params=pltpu.CompilerParams(vmem_limit_bytes=4 * MIB),
        name="pack",
    )(in_hbm(ids), base, in_hbm(moe_tokens))


def join_kernel(keep_ref, came_ref, mark_ref, *out_refs):
    for place, ref in enumerate(out_refs[:-1]):
        ref[0] = keep_ref[place]
        ref[1] = came_ref[place]
    out_refs[-1][...] = mark_ref[...] + 1


def join(keep, came, mark):
    vmem = pl.BlockSpec(memory_space=pltpu.VMEM)
    shape = jax.ShapeDtypeStruct((2,) + keep.shape[1:], keep.dtype)
    count = keep.shape[0]
    return pl.pallas_call(
        join_kernel,
        out_shape=(shape,) * count + (jax.ShapeDtypeStruct(mark.shape, mark.dtype),),
        in_specs=[vmem] * 3,
        out_specs=(vmem,) * (count + 1),
        compiler_params=pltpu.CompilerParams(vmem_limit_bytes=4 * MIB),
        name="join",
    )(keep, came, mark)


def merge_kernel(mark_ref, *refs):
    for place, ref in enumerate(refs[:-1]):
        refs[-1][2 * place : 2 * place + 2] = ref[...]


def merge(mark, pieces):
    vmem = pl.BlockSpec(memory_space=pltpu.VMEM)
    return pl.pallas_call(
        merge_kernel,
        out_shape=jax.ShapeDtypeStruct((2 * len(pieces),) + pieces[0].shape[1:], pieces[0].dtype),
        in_specs=[vmem] * (1 + len(pieces)),
        out_specs=vmem,
        compiler_params=pltpu.CompilerParams(vmem_limit_bytes=4 * MIB),
        name="merge",
    )(mark, *pieces)


def hold_kernel(first, mark_ref, gate_ref, next_ref, held_ref, sems):
    copies = row_copies(gate_ref, first, held_ref, sems)
    for copy in copies:
        copy.start()
    next_ref[...] = mark_ref[...] + 1
    for copy in copies:
        copy.wait()


def hold(mark, gate_weight, first, count):
    vmem = pl.BlockSpec(memory_space=pltpu.VMEM)
    anywhere = pl.BlockSpec(memory_space=pl.ANY)
    columns = gate_weight.shape[1]
    return pl.pallas_call(
        functools.partial(hold_kernel, first),
        out_shape=(jax.ShapeDtypeStruct(mark.shape, mark.dtype), pltpu.VMEM((count, columns), gate_weight.dtype)),
        in_specs=[vmem, anywhere],
        out_specs=(vmem, vmem),
        scratch_shapes=[pltpu.SemaphoreType.DMA((PIECES,))],
        compiler_params=pltpu.CompilerParams(vmem_limit_bytes=MIB),
        cost_estimate=pl.CostEstimate(flops=10**6, bytes_accessed=2 * count * columns, transcendentals=0),
        name="hold",
    )(mark, in_hbm(gate_weight))


def shares_of(ids_ref, tokens_ref, router_ref):
    logits = lax.dot_general(
        router_ref[...], tokens_ref[...], (((1,), (1,)), ((), ())), preferred_element_type=jnp.float32
    )
    places = lax.broadcasted_iota(jnp.int32, logits.shape, 0)
    ids = ids_ref[...]
    picked = [
        jnp.sum(jnp.where(places == ids[pick : pick + 1, :], logits, 0.0), axis=0, keepdims=True)
        for pick in range(TOP)
    ]
    top = jnp.maximum(picked[0], picked[1])
    weights = [jnp.exp(value - top) for value in picked]
    total = weights[0] + weights[1]
    return jnp.concatenate([weights[0] / total, weights[1] / total], axis=0)


def prepare_kernel(
    first, mark_ref, ids_ref, tokens_ref, router_ref, gate_ref, key_ref, value_ref,
    next_ref, shares_ref, pair_ref, held_ref, tokens_vmem, router_vmem, sems, pair_sems,
):
    copies = [
        pltpu.make_async_copy(ref, pair_ref.at[place], pair_sems.at[place])
        for place, ref in enumerate((key_ref, value_ref))
    ] + row_copies(gate_ref, first, held_ref, sems)
    small = [
        pltpu.make_async_copy(tokens_ref, tokens_vmem, pair_sems.at[2]),
        pltpu.make_async_copy(router_ref, router_vmem, pair_sems.at[3]),
    ]
    for copy in small + copies:
        copy.start()
    next_ref[...] = mark_ref[...] + 1
    for copy in small:
        copy.wait()
    shares_ref[...] = shares_of(ids_ref, tokens_vmem, router_vmem)
    for copy in copies:
        copy.wait()


def prepare(mark, ids, moe_tokens, router_weight, gate_weight, keys, values, first, count):
    vmem = pl.BlockSpec(memory_space=pltpu.VMEM)
    anywhere = pl.BlockSpec(memory_space=pl.ANY)
    columns = gate_weight.shape[1]
    return pl.pallas_call(
        functools.partial(prepare_kernel, first),
        out_shape=(
            jax.ShapeDtypeStruct(mark.shape, mark.dtype),
            jax.ShapeDtypeStruct(ids.shape, jnp.float32),
            jax.ShapeDtypeStruct((2,) + keys.shape, keys.dtype),
            pltpu.VMEM((count, columns), gate_weight.dtype),
        ),
        in_specs=[vmem] * 2 + [anywhere] * 5,
        out_specs=(vmem, vmem, anywhere, vmem),
        scratch_shapes=[
            pltpu.VMEM(moe_tokens.shape, moe_tokens.dtype),
            pltpu.VMEM(router_weight.shape[::-1], router_weight.dtype),
            pltpu.SemaphoreType.DMA((PIECES,)),
            pltpu.SemaphoreType.DMA((4,)),
        ],
        compiler_params=pltpu.CompilerParams(vmem_limit_bytes=2 * MIB),
        cost_estimate=pl.CostEstimate(flops=10**6, bytes_accessed=2 * count * columns, transcendentals=0),
        name="prepare",
    )(mark, *map(in_hbm, (ids, moe_tokens, router_weight.T, gate_weight, keys, values)))


def experts_kernel(helds, base_ref, near_ref, far_ref, *refs):
    gate_refs, refs = refs[:helds], refs[helds:]
    gate_ref, up_ref, down_ref, mine_ref, other_ref, parts_ref, rows_ref, sums_ref, gate_vmem, up_vmem, down_vmem, sems = refs
    senders = mine_ref.shape[0]
    count = 2 * senders * CAP
    chunks = up_ref.shape[1] // HIDDEN_CHUNK
    depth = down_vmem.shape[0]

    def span(chunk):
        return pl.ds(pl.multiple_of(chunk * HIDDEN_CHUNK, HIDDEN_CHUNK), HIDDEN_CHUNK)

    def gate_copy(chunk, slot):
        rest = pl.ds(STREAMED_FROM, D - STREAMED_FROM)
        return pltpu.make_async_copy(gate_ref.at[rest, span(chunk)], gate_vmem.at[slot], sems.at[2, slot])

    def up_copy(chunk, slot):
        return pltpu.make_async_copy(up_ref.at[:, span(chunk)], up_vmem.at[slot], sems.at[0, slot])

    def down_copy(chunk, slot):
        return pltpu.make_async_copy(down_ref.at[span(chunk)], down_vmem.at[slot], sems.at[1, slot])

    for chunk in range(min(depth, chunks)):
        gate_copy(chunk, chunk).start()
        up_copy(chunk, chunk).start()
        down_copy(chunk, chunk).start()
    for place, ref in enumerate((near_ref, far_ref)):
        here = ref.shape[0]

        def unpack(i, carry, place=place, ref=ref, here=here):
            first = pl.multiple_of((place * here + i) * CAP * PARTS, 8)
            parts_ref[pl.ds(first, CAP * PARTS), :] = (
                ref[i].astype(jnp.float32).reshape(CAP * PARTS, PART_WIDTH)
            )
            return carry

        lax.fori_loop(0, here, unpack, 0)
    for part in range(PARTS):
        columns = slice(part * PART_WIDTH, (part + 1) * PART_WIDTH)
        rows_ref[:, columns] = parts_ref[pl.ds(part, count, stride=PARTS), :].astype(jnp.bfloat16)

    def work(chunk, first):
        slot = lax.rem(chunk, depth)
        gate_value, first_row = None, 0
        for ref in gate_refs:
            part = jnp.dot(
                rows_ref[:, first_row : first_row + ref.shape[0]], ref[:, span(chunk)], preferred_element_type=jnp.float32
            )
            gate_value = part if gate_value is None else gate_value + part
            first_row += ref.shape[0]
        gate_copy(chunk, slot).wait()
        gate_value += jnp.dot(rows_ref[:, STREAMED_FROM:], gate_vmem[slot], preferred_element_type=jnp.float32)
        up_copy(chunk, slot).wait()
        up_value = jnp.dot(rows_ref[...], up_vmem[slot], preferred_element_type=jnp.float32)
        hidden = (gate_value / (1.0 + jnp.exp(-gate_value)) * up_value).astype(jnp.bfloat16)

        @pl.when(chunk + depth < chunks)
        def _():
            gate_copy(chunk + depth, slot).start()
            up_copy(chunk + depth, slot).start()

        down_copy(chunk, slot).wait()
        product = jnp.dot(hidden, down_vmem[slot], preferred_element_type=jnp.float32)
        if first:
            sums_ref[...] = product
        else:
            sums_ref[...] += product

        @pl.when(chunk + depth < chunks)
        def _():
            down_copy(chunk + depth, slot).start()

    work(jnp.int32(0), True)

    def step(chunk, carry):
        work(chunk, False)
        return carry

    lax.fori_loop(1, chunks, step, 0)
    for part in range(PARTS):
        columns = slice(part * PART_WIDTH, (part + 1) * PART_WIDTH)
        parts_ref[pl.ds(part, count, stride=PARTS), :] = sums_ref[:, columns]

    def give(i, carry):
        first = pl.multiple_of(i * CAP * PARTS, 8)
        sender = lax.bitwise_xor(jnp.int32(i), base_ref[0])
        mine_ref[sender] = parts_ref[pl.ds(first, CAP * PARTS), :].reshape(CAP, PARTS, PART_WIDTH)
        second = pl.multiple_of((senders + i) * CAP * PARTS, 8)
        other_ref[sender] = (
            parts_ref[pl.ds(second, CAP * PARTS), :].reshape(CAP, PARTS, PART_WIDTH).astype(jnp.bfloat16)
        )
        return carry

    lax.fori_loop(0, senders, give, 0)


def experts(base, near, far, gate_held, gate_weight, up_weight, down_weight):
    shape = near.shape
    count = 2 * shape[0] * CAP
    smem = pl.BlockSpec(memory_space=pltpu.SMEM)
    vmem = pl.BlockSpec(memory_space=pltpu.VMEM)
    anywhere = pl.BlockSpec(memory_space=pl.ANY)
    depth = min(3, up_weight.shape[1] // HIDDEN_CHUNK)
    return pl.pallas_call(
        functools.partial(experts_kernel, len(gate_held)),
        out_shape=(pltpu.VMEM(shape, jnp.float32), pltpu.VMEM(shape, jnp.bfloat16)),
        in_specs=[smem] + [vmem] * (2 + len(gate_held)) + [anywhere] * 3,
        out_specs=(vmem, vmem),
        scratch_shapes=[
            pltpu.VMEM((count * PARTS, PART_WIDTH), jnp.float32),
            pltpu.VMEM((count, D), jnp.bfloat16),
            pltpu.VMEM((count, D), jnp.float32),
            pltpu.VMEM((depth, D - STREAMED_FROM, HIDDEN_CHUNK), jnp.bfloat16),
            pltpu.VMEM((depth, D, HIDDEN_CHUNK), jnp.bfloat16),
            pltpu.VMEM((depth, HIDDEN_CHUNK, D), jnp.bfloat16),
            pltpu.SemaphoreType.DMA((3, depth)),
        ],
        compiler_params=pltpu.CompilerParams(vmem_limit_bytes=32 * MIB),
        cost_estimate=SMALL_COST,
        name="experts",
    )(
        base,
        in_vmem(near),
        in_vmem(far),
        *map(in_vmem, gate_held),
        in_hbm(gate_weight),
        in_hbm(up_weight),
        in_hbm(down_weight),
    )


def add_kernel(mine_ref, other_ref, sum_ref, mark_ref):
    sum_ref[...] = (mine_ref[...] + other_ref[...].astype(jnp.float32)).astype(jnp.bfloat16)
    mark_ref[...] = jnp.zeros_like(mark_ref)


def add(mine, other):
    vmem = pl.BlockSpec(memory_space=pltpu.VMEM)
    return pl.pallas_call(
        add_kernel,
        out_shape=(jax.ShapeDtypeStruct(mine.shape, jnp.bfloat16), jax.ShapeDtypeStruct((8, 128), jnp.float32)),
        in_specs=[vmem, vmem],
        out_specs=(vmem, vmem),
        compiler_params=pltpu.CompilerParams(vmem_limit_bytes=24 * MIB),
        name="add",
    )(mine, other)


def follow_kernel(mark_ref, *refs):
    del mark_ref, refs


def follow(mark, arrays):
    anywhere = pl.BlockSpec(memory_space=pl.ANY)
    return pl.pallas_call(
        follow_kernel,
        out_shape=tuple(jax.ShapeDtypeStruct(x.shape, x.dtype) for x in arrays),
        in_specs=[anywhere] * (1 + len(arrays)),
        out_specs=(anywhere,) * len(arrays),
        input_output_aliases={1 + i: i for i in range(len(arrays))},
        compiler_params=pltpu.CompilerParams(vmem_limit_bytes=MIB),
        name="follow",
    )(mark, *arrays)


def combine_kernel(ids_ref, shares_ref, back_ref, attended_ref, out_ref, rows_ref, count_ref):
    del attended_ref
    tokens = out_ref.shape[0]
    holders = back_ref.shape[0] // EXPERTS
    for expert in range(EXPERTS):
        count_ref[expert] = 0
    for token in range(tokens):
        total = None
        for pick in range(TOP):
            expert = ids_ref[pick, token]
            slot = count_ref[expert]
            count_ref[expert] = slot + 1
            value = back_ref[expert * holders, slot].astype(jnp.float32)
            for holder in range(1, holders):
                value += back_ref[expert * holders + holder, slot].astype(jnp.float32)
            value = shares_ref[pick, token] * value
            total = value if total is None else total + value
        rows_ref[token * PARTS : (token + 1) * PARTS, :] = total
    for part in range(PARTS):
        columns = slice(part * PART_WIDTH, (part + 1) * PART_WIDTH)
        out_ref[:, columns] = rows_ref[pl.ds(part, tokens, stride=PARTS), :].astype(jnp.bfloat16)


def combine(ids, gate_shares, back, attended):
    tokens = ids.shape[1]
    smem = pl.BlockSpec(memory_space=pltpu.SMEM)
    vmem = pl.BlockSpec(memory_space=pltpu.VMEM)
    return pl.pallas_call(
        combine_kernel,
        out_shape=jax.ShapeDtypeStruct((tokens, D), jnp.bfloat16),
        in_specs=[smem, smem, vmem, pl.BlockSpec(memory_space=pl.ANY)],
        out_specs=vmem,
        scratch_shapes=[
            pltpu.VMEM((tokens * PARTS, PART_WIDTH), jnp.float32),
            pltpu.SMEM((EXPERTS,), jnp.int32),
        ],
        compiler_params=pltpu.CompilerParams(vmem_limit_bytes=16 * MIB),
        name="combine",
    )(ids, gate_shares, back, in_hbm(attended))


def attention_kernel(
    place_ref, lists_ref, query_ref, b0, b1, b2, b3, b4, b5, out_ref, staged, scores, weights, done, sems
):
    blocks = (b0, b1, b2, b3, b4, b5)
    tiles_here = query_ref.shape[0] // TILE_POSITIONS
    steps = KEY_VALUE_HEADS // HEADS_PER_STEP
    step_width = HEADS_PER_STEP * QUERY_PER_GROUP * HEAD_SIZE
    rounds = tiles_here * steps

    head_width = QUERY_PER_GROUP * HEAD_SIZE

    def out_copy(turn, slot, head):
        rows = pl.ds(pl.multiple_of(lax.div(turn, steps) * TILE_POSITIONS, TILE_POSITIONS), TILE_POSITIONS)
        first = lax.rem(turn, steps) * step_width + head * head_width
        return pltpu.make_async_copy(
            done.at[slot, :, pl.ds(head * head_width, head_width)],
            out_ref.at[rows, pl.ds(pl.multiple_of(first, head_width), head_width)],
            sems.at[slot, head],
        )

    def gather(tile, count):
        def one(entry):
            relative = jnp.clip(lists_ref[tile, entry] - place_ref[0], 0, (PRIOR_DEVICES + 1) * tiles_here - 1)
            source = place_ref[1 + lax.div(relative, tiles_here)]
            first = pl.multiple_of(lax.rem(relative, tiles_here) * TILE_POSITIONS, TILE_POSITIONS)
            for number, block in enumerate(blocks):

                @pl.when(source == number)
                def _(block=block):
                    for which in range(2):
                        staged[which, entry * TILE_POSITIONS : (entry + 1) * TILE_POSITIONS, :] = block[
                            which, pl.ds(first, TILE_POSITIONS), :
                        ]

        for entry in range(MOST_LISTED):
            pl.when(entry < count)(functools.partial(one, entry))

    def turn_body(turn, carry):
        tile, step = lax.div(turn, steps), lax.rem(turn, steps)
        slot = lax.rem(turn, 2)
        count = jnp.int32(1)
        for entry in range(1, MOST_LISTED):
            count += (lists_ref[tile, entry] >= 0).astype(jnp.int32)
        pl.when(step == 0)(functools.partial(gather, tile, count))

        @pl.when(turn >= 2)
        def _():
            for head in range(HEADS_PER_STEP):
                out_copy(turn - 2, slot, head).wait()

        for listed in range(1, MOST_LISTED + 1):
            pl.when(count == listed)(functools.partial(attend, turn, slot, listed))
        return carry

    def attend(turn, slot, listed):
        tile, step = lax.div(turn, steps), lax.rem(turn, steps)
        query_rows = pl.ds(pl.multiple_of(tile * TILE_POSITIONS, TILE_POSITIONS), TILE_POSITIONS)
        width = listed * TILE_POSITIONS
        units = [(head, part) for head in range(HEADS_PER_STEP) for part in range(2)]
        group_count = QUERY_PER_GROUP // 2
        row_place = lax.broadcasted_iota(jnp.int32, (TILE_POSITIONS, TILE_POSITIONS), 0)
        column_place = lax.broadcasted_iota(jnp.int32, (TILE_POSITIONS, TILE_POSITIONS), 1)
        causal = column_place <= row_place
        totals = {}

        def first_column(unit, group):
            head, part = units[unit]
            return (head * QUERY_PER_GROUP + part * group_count + group) * HEAD_SIZE

        def query(unit, group):
            first = pl.multiple_of(step * step_width + first_column(unit, group), HEAD_SIZE)
            return query_ref[query_rows, pl.ds(first, HEAD_SIZE)]

        def head_columns(unit):
            return pl.ds(pl.multiple_of((step * HEADS_PER_STEP + units[unit][0]) * HEAD_SIZE, HEAD_SIZE), HEAD_SIZE)

        def score(unit):
            rows = jnp.concatenate([query(unit, group) for group in range(group_count)], axis=0)
            keys = staged[0, :width, head_columns(unit)]
            scores[unit, :, :width] = lax.dot_general(
                rows, keys, (((1,), (1,)), ((), ())), preferred_element_type=jnp.float32
            )

        def weigh(unit):
            for group in range(group_count):
                rows = slice(group * TILE_POSITIONS, (group + 1) * TILE_POSITIONS)
                blocks = [jnp.where(causal, scores[unit, rows, :TILE_POSITIONS], -1e30)]
                blocks += [
                    scores[unit, rows, entry * TILE_POSITIONS : (entry + 1) * TILE_POSITIONS]
                    for entry in range(1, listed)
                ]
                top = blocks[0]
                for block in blocks[1:]:
                    top = jnp.maximum(top, block)
                top = jnp.max(top, axis=1, keepdims=True)
                total = None
                for entry, block in enumerate(blocks):
                    weight = jnp.exp2((block - top) * (HEAD_SIZE**-0.5 * LOG2_E))
                    total = weight if total is None else total + weight
                    weights[unit, rows, entry * TILE_POSITIONS : (entry + 1) * TILE_POSITIONS] = weight.astype(
                        jnp.bfloat16
                    )
                totals[unit, group] = 1.0 / jnp.sum(total, axis=1, keepdims=True)

        def finish(unit):
            values = staged[1, :width, head_columns(unit)]
            summed = jnp.dot(weights[unit, :, :width], values, preferred_element_type=jnp.float32)
            for group in range(group_count):
                rows = slice(group * TILE_POSITIONS, (group + 1) * TILE_POSITIONS)
                first = first_column(unit, group)
                done[slot, :, first : first + HEAD_SIZE] = (summed[rows] * totals[unit, group]).astype(jnp.bfloat16)

        for stage in range(len(units) + 2):
            if stage < len(units):
                score(stage)
            if 0 <= stage - 2:
                finish(stage - 2)
                if units[stage - 2][1] == 1:
                    out_copy(turn, slot, units[stage - 2][0]).start()
            if 0 <= stage - 1 < len(units):
                weigh(stage - 1)

    lax.fori_loop(0, rounds, turn_body, 0)
    for turn in range(max(rounds - 2, 0), rounds):
        for head in range(HEADS_PER_STEP):
            out_copy(jnp.int32(turn), turn % 2, head).wait()


def attention(place, tile_lists, queries, blocks):
    smem = pl.BlockSpec(memory_space=pltpu.SMEM)
    vmem = pl.BlockSpec(memory_space=pltpu.VMEM)
    unit = (2 * HEADS_PER_STEP, QUERY_PER_GROUP // 2 * TILE_POSITIONS, MOST_LISTED * TILE_POSITIONS)
    return pl.pallas_call(
        attention_kernel,
        out_shape=jax.ShapeDtypeStruct(queries.shape, jnp.bfloat16),
        in_specs=[smem, smem] + [vmem] * 7,
        out_specs=pl.BlockSpec(memory_space=pl.ANY),
        scratch_shapes=[
            pltpu.VMEM((2, MOST_LISTED * TILE_POSITIONS, KEY_VALUE_HEADS * HEAD_SIZE), jnp.bfloat16),
            pltpu.VMEM(unit, jnp.float32),
            pltpu.VMEM(unit, jnp.bfloat16),
            pltpu.VMEM((2, TILE_POSITIONS, HEADS_PER_STEP * QUERY_PER_GROUP * HEAD_SIZE), jnp.bfloat16),
            pltpu.SemaphoreType.DMA((2, HEADS_PER_STEP)),
        ],
        compiler_params=pltpu.CompilerParams(vmem_limit_bytes=32 * MIB),
        cost_estimate=SMALL_COST,
        name="attention",
    )(place, tile_lists, queries, *blocks)


def shards(
    queries,
    key_matrix,
    value_matrix,
    tile_lists,
    moe_tokens,
    expert_ids,
    router_weight,
    gate_weight,
    up_weight,
    down_weight,
):
    devices = lax.axis_size("ctx")
    me = lax.axis_index("ctx")
    ids = expert_ids.T
    direct = devices == 2 * EXPERTS
    base = (me // 2 if direct else jnp.zeros_like(me)).astype(jnp.int32)[None]
    gate_held = []
    keep, send = pack(ids, base, moe_tokens)
    mark = jnp.zeros((8, 128), jnp.float32)
    rest = (ids, moe_tokens, router_weight, gate_weight, key_matrix, value_matrix)
    if direct:
        came = exchanged(send, 2)
        mark, held = hold(mark, gate_weight, 0, HELD_ROWS[0])
        gate_held.append(held)
        *pieces, mark = join(keep, came, mark)
        pieces[1:] = [exchanged(pieces[place], 4 * place) for place in range(1, len(pieces))]
        mark, gate_shares, own, held = prepare(mark, *rest, HELD_ROWS[0], HELD_ROWS[1])
        near = merge(mark, pieces)
    else:
        packed = jnp.stack([keep, send], axis=1).reshape((EXPERTS,) + keep.shape[1:])
        near = same_core_exchange(jnp.repeat(packed, devices // (2 * EXPERTS), axis=0))
        mark, gate_shares, own, held = prepare(mark, *rest, 0, STREAMED_FROM)
    gate_held.append(held)
    far = exchanged(near, 1)
    two_before = passed_along(own, 2)
    four_before = passed_along(own, 4)
    mine, other = experts(base, near, far, gate_held, gate_weight, up_weight, down_weight)
    summed, mark = add(mine, exchanged(other, 1))
    back = same_core_exchange(summed)
    blocks = list(follow(mark, [own, two_before, four_before]))
    blocks += [exchanged(x, 1) for x in blocks]
    tiles_here = queries.shape[0] // TILE_POSITIONS
    sources = jnp.where(me % 2 == 0, *(jnp.array(row, jnp.int32) for row in WINDOW_SOURCES))
    place = jnp.concatenate([((me - PRIOR_DEVICES) * tiles_here).astype(jnp.int32)[None], sources])
    attended = attention(place, tile_lists, queries, blocks)
    combined = combine(ids, gate_shares, back, attended)
    return (attended, combined)


def solution(mesh):
    split = P(("group", "ctx"), None)
    placed = (split, split, split, split, split, split, P(), P(None, "ctx"), P(None, "ctx"), P("ctx", None))
    return jax.shard_map(shards, mesh=mesh, in_specs=placed, out_specs=(split, split), check_vma=False)
```
